32 devices in a mesh: rep: 2 (over x), section: 2 (over core), tp: 8 (over z, y).
Axes of the slice: x: 2, y: 2, z: 4, core: 2. Of those that a mesh axis runs over, the one named last changes fastest.
Arguments:
- queries: bfloat16 [2, 16, 64, 128], P('section', 'rep', 'tp'), parts along dimension 1, may hold values from -200 to 200
- new_kv: bfloat16 [2, 16, 2, 4, 128], P('section', 'rep'), parts along dimension 1, may hold values from -6 to 6
- kv_cache: bfloat16 [2, 16, 2, 4, 1024, 128], P('section', 'rep', None, None, 'tp'), parts along dimension 1, may hold values from -6 to 6
- lengths: int32 [2, 16], P('section', 'rep'), parts along dimension 1, may hold values from 2 to 1023, as said below
- residual: bfloat16 [2, 16, 16384], P('section', 'rep', 'tp'), parts along dimension 1, may hold values from -3 to 3
- out_weight: bfloat16 [2, 8192, 16384], P('section', 'tp'), may hold values from -0.09375 to 0.09375
Outputs:
- handed: bfloat16 [2, 16, 16384], P('section', 'rep'), parts along dimension 1
The draws below stay inside these ranges and needn't reach their ends.
There are 2 independent parts, one for each index of `rep`. The reference program is written for one: setup_inputs(seed, part) draws one part's arguments, and reference() takes and returns one part's arrays. A program takes and returns all parts, laid end to end along the dimension named above; an argument that names none is the same for every part. Nothing has to cross between parts.
Inputs may be any that keep to these rules, and one draw needn't show every extreme that they name: Row r attends to cached positions 0 to lengths - 1 and to its new token at position lengths; in each section some row has the largest value.
All inputs are finite; a program needn't handle non-finite values.
Results may differ from the reference program's by a relative error of at most 0.039.
Values may be sent and summed in bfloat16 or wider, within the bound.
No kernel may reach another device: no remote copies, remote signals or barrier semaphores. Data moves between devices by JAX's collectives and lax.ppermute only.
A program may use at most 192 MiB of HBM per device.

```python
import math
import jax
import jax.numpy as jnp
from jax import lax

D = 16384
HQ = 64
KVH = 4
HD = 128
QB = 128
ROWS = 8
SECTIONS = 2
LEN = 1024
N_TP = 8


def lead_keys(key):
    drawn = jax.random.normal(key, (SECTIONS, ROWS, KVH, HD), jnp.float32)
    return jnp.clip(drawn, -6.0, 6.0)


def draw_kv_cache(key, part):
    first_block = lead_keys(key)
    key = jax.random.fold_in(key, 11)
    stored = jax.random.normal(key, (SECTIONS, ROWS, 2, KVH, LEN, HD), jnp.float32)
    stored = jnp.clip(stored, -6.0, 6.0)
    stored = stored.at[:, :, 0, :, 0, :].set(first_block)
    return stored.astype(jnp.bfloat16)


def draw_queries(key, part):
    key = jax.random.fold_in(key, 5)
    drawn = jnp.clip(2.5 * jax.random.normal(key, (SECTIONS, ROWS, HQ, HD), jnp.float32), -15.0, 15.0)
    return drawn.astype(jnp.bfloat16)


def draw_new_kv(key, part):
    key = jax.random.fold_in(key, 7)
    drawn = jnp.clip(jax.random.normal(key, (SECTIONS, ROWS, 2, KVH, HD), jnp.float32), -6.0, 6.0)
    return drawn.astype(jnp.bfloat16)


def draw_residual(key, part):
    key = jax.random.fold_in(key, 9)
    drawn = jnp.clip(0.5 * jax.random.normal(key, (SECTIONS, ROWS, D), jnp.float32), -3.0, 3.0)
    return drawn.astype(jnp.bfloat16)


def draw_lengths(key, part):
    key = jax.random.fold_in(key, 3)
    first_key, second_key = jax.random.split(key)
    drawn = jax.random.randint(first_key, (SECTIONS, ROWS), 2, LEN)
    longest = jax.random.randint(second_key, (SECTIONS, 1), 0, ROWS)
    return jnp.where(jnp.arange(ROWS)[None, :] == longest, LEN - 1, drawn).astype(jnp.int32)


def strengthened(entries, rng, source, target, parts, factor):
    def block_of(axis_at):
        return (jnp.arange(entries.shape[axis_at]) // (entries.shape[axis_at] // parts)).reshape((-1,) + (1,) * (entries.ndim - 1 - axis_at))

    near = jax.random.permutation(rng, parts)[block_of(target)]
    second = (block_of(target) + parts // 2) % parts
    return jnp.where((block_of(source) == near) | (block_of(source) == second), factor * entries, entries)


def level_of(rng, shape, cuts, least, top_value):
    gain, own = 1.0, jax.random.fold_in(rng, 6)
    for dim, parts in cuts:
        heights = jnp.exp(jax.random.uniform(jax.random.fold_in(own, dim), (parts,), jnp.float32, least / len(cuts), top_value / len(cuts)))
        gain = gain * jnp.repeat(heights, shape[dim] // parts).reshape([-1 if axis == dim else 1 for axis in range(len(shape))])
    return gain


def bell_draw_with(key, dims, width, limit, cuts, heavy, kind=jnp.bfloat16):
    entries = width * jax.random.normal(key, dims, jnp.float32)
    if cuts:
        entries = entries * level_of(key, dims, cuts, -0.22, 0.18)
    return jnp.clip(strengthened(entries, jax.random.fold_in(key, 3), *heavy), -limit, limit).astype(kind)


def setup_inputs(seed: int = 0, part: int = 0) -> dict:
    seeds = jax.random.split(jax.random.key(seed), 7)
    own_keys = jax.random.split(jax.random.fold_in(seeds[6], part), 7)
    return {
        "queries": draw_queries(jax.random.fold_in(jax.random.fold_in(seeds[6], part), 71), part),
        "new_kv": draw_new_kv(jax.random.fold_in(jax.random.fold_in(seeds[6], part), 71), part),
        "kv_cache": draw_kv_cache(jax.random.fold_in(jax.random.fold_in(seeds[6], part), 71), part),
        "lengths": draw_lengths(jax.random.fold_in(jax.random.fold_in(seeds[6], part), 71), part),
        "residual": draw_residual(jax.random.fold_in(jax.random.fold_in(seeds[6], part), 71), part),
        "out_weight": bell_draw_with(seeds[5], (SECTIONS, HQ * HD, D), (HQ * HD) ** -0.5, 0.09375, ((0, 2), (1, 8)), (1, 2, 8, 2.0)),
    }


def block_scale(blocks):
    return ((lax.optimization_barrier(jnp.max(jnp.abs(blocks), axis=-1)) + 1e-06) / 127.0).astype(jnp.bfloat16)

def quantize(blocks, scale_wide):
    return jnp.clip(jnp.floor(blocks / scale_wide[..., None] + 0.5), -127.0, 127.0).astype(jnp.bfloat16)

def head_block(operands):
    return jnp.dot(operands[0], operands[1], preferred_element_type=jnp.float32)

def section_layer(query_rows, new_rows, cache_rows, length, residual_rows, weight_rows):
    positions = jnp.arange(LEN, dtype=jnp.int32)
    written = positions[None, :] == length[:, None]
    stored = jnp.where(written[:, None, None, :, None], new_rows[:, :, :, None, :], cache_rows)
    key_cache = stored[:, 0].astype(jnp.float32)
    value_cache = stored[:, 1].astype(jnp.float32)
    grouped = query_rows.reshape(ROWS, KVH, HQ // KVH, HD).astype(jnp.float32)
    scores = jnp.einsum('rkgd,rkpd->rkgp', grouped, key_cache) * (1.0 / math.sqrt(HD))
    visible = (positions[None, :] <= length[:, None])[:, None, None, :]
    scores = jnp.where(visible, scores, -1e+30)
    top_score = lax.optimization_barrier(jnp.max(scores, axis=-1))
    weights = jnp.where(visible, jnp.exp(scores - top_score[..., None]), 0.0)
    totals = lax.optimization_barrier(jnp.sum(weights, axis=-1))
    rounded = weights.astype(jnp.bfloat16).astype(jnp.float32)
    mixed = jnp.einsum('rkgp,rkpd->rkgd', rounded, value_cache)
    attended = (mixed / totals[..., None]).astype(jnp.bfloat16)
    attended = attended.reshape(ROWS, N_TP, HQ // N_TP * HD).transpose(1, 0, 2)
    weight_blocks = weight_rows.reshape(N_TP, HQ // N_TP * HD, D)
    partials = lax.map(head_block, (attended, weight_blocks))
    blocks = partials.reshape(N_TP, ROWS, D // QB, QB)
    scales = block_scale(blocks)
    scale_wide = lax.optimization_barrier(scales).astype(jnp.float32)
    levels = quantize(blocks, scale_wide)
    summed = lax.optimization_barrier(jnp.sum(levels.astype(jnp.float32) * scale_wide[..., None], axis=0))
    summed = residual_rows.astype(jnp.float32).reshape(ROWS, D // QB, QB) + summed
    scales_out = block_scale(summed)
    scales_out_wide = lax.optimization_barrier(scales_out).astype(jnp.float32)
    levels_out = quantize(summed, scales_out_wide)
    output = (levels_out.astype(jnp.float32) * scales_out_wide[..., None]).astype(jnp.bfloat16)
    return output.reshape(ROWS, D)

def reference(queries, new_kv, kv_cache, lengths, residual, out_weight):
    outputs = []
    for section_index in range(SECTIONS):
        outputs.append(section_layer(queries[section_index], new_kv[section_index], kv_cache[section_index], lengths[section_index], residual[section_index], out_weight[section_index]))
    stacked = jnp.stack(outputs, axis=0)
    return jnp.roll(stacked, 1, axis=0)
```

```python
import functools
import math

import jax
import jax.numpy as jnp
from jax import lax
from jax.experimental import pallas as pl
from jax.experimental.pallas import tpu as pltpu
from jax.sharding import PartitionSpec as P

QB = 128
LANES = 128
STAT_ROWS = 16
MIB = 1 << 20
F32 = jnp.float32
BF16 = jnp.bfloat16


def exchanged(array, k, tp, sections, shift):
    pairs = [
        (s * tp + t, ((s + shift) % sections) * tp + (t ^ k))
        for s in range(sections)
        for t in range(tp)
    ]
    return lax.ppermute(array, ("section", "tp"), pairs)


def pieces(x):
    high = x.astype(BF16).astype(F32)
    rest = x - high
    middle = rest.astype(BF16).astype(F32)
    return high, middle, rest - middle


def attention_kernel(tp, group, lengths_ref, new_ref, kv_ref, *refs):
    queries, outs = refs[:tp], refs[tp : 2 * tp]
    scores_ref, mixed_ref = refs[2 * tp :]
    rows, heads = queries[0].shape[1:3]
    kv_heads, span, dim = kv_ref.shape[3:]
    per = group // heads
    rank = lax.axis_index("tp")
    first = rank * span
    scale = 1.0 / math.sqrt(dim)
    sub = lax.broadcasted_iota(jnp.int32, (span, dim), 0)
    kv_sub = lax.broadcasted_iota(jnp.int32, (kv_heads, dim), 0)

    def cached(r, which, kv_head):
        new = new_ref[0, r, which].astype(F32)
        new = jnp.sum(jnp.where(kv_sub == kv_head, new, 0.0), axis=0, keepdims=True)
        block = kv_ref[0, r, which, kv_head]
        return jnp.where(sub == lengths_ref[0, r] - first, new, block.astype(F32)).astype(BF16)

    for m in range(kv_heads):
        kv_head = (rank // per) ^ m
        for r in range(rows):
            q = jnp.concatenate(
                [queries[m * per + i][0, r].astype(F32) for i in range(per)], axis=0
            ).astype(BF16)
            keys = cached(r, 0, kv_head)
            s = lax.dot_general(q, keys, (((1,), (1,)), ((), ())), preferred_element_type=F32)
            scores_ref[m * group : (m + 1) * group, r, :] = s * scale

    row_of = lax.broadcasted_iota(jnp.int32, (rows, span), 0)
    pos = lax.broadcasted_iota(jnp.int32, (rows, span), 1) + first
    limit = jnp.zeros((rows, span), jnp.int32)
    for r in range(rows):
        limit = jnp.where(row_of == r, lengths_ref[0, r], limit)
    visible = (pos <= limit)[None]
    scores = jnp.where(visible, scores_ref[...], -1e30)
    top = jnp.max(scores, axis=-1, keepdims=True)
    weights = jnp.where(visible, jnp.exp(scores - top), 0.0)
    total = jnp.sum(weights, axis=-1, keepdims=True)
    scores_ref[...] = weights

    for m in range(kv_heads):
        kv_head = (rank // per) ^ m
        for r in range(rows):
            w = scores_ref[m * group : (m + 1) * group, r, :].astype(BF16)
            values = cached(r, 1, kv_head)
            mixed_ref[m * group : (m + 1) * group, r, :] = jnp.dot(
                w, values, preferred_element_type=F32
            )

    n = heads * rows
    sub_n = lax.broadcasted_iota(jnp.int32, (n, LANES), 0)
    lane_n = lax.broadcasted_iota(jnp.int32, (n, LANES), 1)
    stat_sub = lax.broadcasted_iota(jnp.int32, (STAT_ROWS, LANES), 0)
    for k in range(tp):
        own = slice(k * heads, (k + 1) * heads)
        outs[k][:n, :] = mixed_ref[own].reshape(n, dim).astype(BF16)
        tops = jnp.where(lane_n == sub_n, top[own].reshape(n, 1), 0.0)
        sums = jnp.where(lane_n == sub_n + n, total[own].reshape(n, 1), 0.0)
        stats = jnp.sum(tops + sums, axis=0, keepdims=True)
        tile = jnp.zeros((STAT_ROWS, LANES), F32)
        for i, piece in enumerate(pieces(stats)):
            tile = jnp.where(stat_sub == i, piece, tile)
        outs[k][n:, :] = tile.astype(BF16)


def attended_block(blocks, rows, heads):
    n = rows * heads
    sub_n = lax.broadcasted_iota(jnp.int32, (n, LANES), 0)
    lane_n = lax.broadcasted_iota(jnp.int32, (n, LANES), 1)
    tops, sums = [], []
    for block in blocks:
        tile = block[n:, :].astype(F32)
        stats = tile[0:1] + tile[1:2] + tile[2:3]
        tops.append(jnp.sum(jnp.where(lane_n == sub_n, stats, 0.0), axis=1, keepdims=True))
        sums.append(jnp.sum(jnp.where(lane_n == sub_n + n, stats, 0.0), axis=1, keepdims=True))
    overall = functools.reduce(jnp.maximum, tops)
    total = jnp.zeros((n, 1), F32)
    mixed = jnp.zeros((n, LANES), F32)
    for block, top, part in zip(blocks, tops, sums):
        factor = jnp.exp(top - overall)
        total = total + part * factor
        mixed = mixed + block[:n, :].astype(F32) * factor
    attended = mixed / total
    return jnp.concatenate(
        [attended[h * rows : (h + 1) * rows] for h in range(heads)], axis=1
    ).astype(BF16)


def requantized(x):
    top = jnp.max(jnp.abs(x), axis=-1, keepdims=True)
    scale = ((top + 1e-06) / 127.0).astype(BF16).astype(F32)
    return jnp.clip(jnp.floor(x / scale + 0.5), -127.0, 127.0) * scale


def projection_kernel(tp, rows, heads, tile, weight_ref, *refs):
    blocks, outs = refs[:tp], refs[tp : 2 * tp]
    held, sems = refs[2 * tp :]
    rank = lax.axis_index("tp")
    width = outs[0].shape[1]
    order = list(range(tp))[::-1]

    def copy(k):
        start = pl.multiple_of((rank ^ k) * width, width)
        return pltpu.make_async_copy(
            weight_ref.at[0, :, pl.ds(start, width)], held.at[k], sems.at[k]
        )

    for k in order:
        copy(k).start()
    flat = attended_block(blocks, rows, heads)
    for k in order:
        copy(k).wait()
        for c in range(width // tile):
            part = jnp.dot(
                flat, held[k, :, c * tile : (c + 1) * tile], preferred_element_type=F32
            )
            for b in range(tile // QB):
                at = c * tile + b * QB
                outs[k][:, at : at + QB] = requantized(part[:, b * QB : (b + 1) * QB]).astype(BF16)


def sum_kernel(tp, residual_ref, *refs):
    parts, out_ref = refs[:tp], refs[tp]
    for b in range(out_ref.shape[1] // QB):
        at = slice(b * QB, (b + 1) * QB)
        x = functools.reduce(lambda a, c: a + c, [part[:, at].astype(F32) for part in parts])
        x = x + residual_ref[0, :, at].astype(F32)
        out_ref[:, at] = requantized(x).astype(BF16)


def place_kernel(tp, *refs):
    blocks, out_ref = refs[:tp], refs[tp]
    width = blocks[0].shape[1]
    rank = lax.axis_index("tp")
    for k in range(tp):
        start = pl.multiple_of((rank ^ k) * width, width)
        out_ref[0, :, pl.ds(start, width)] = blocks[k][...]


def params(mib):
    return pltpu.CompilerParams(vmem_limit_bytes=mib * MIB)


def local(tp, sections, queries, new_kv, kv_cache, lengths, residual, out_weight):
    rows, heads, dim = queries.shape[1:]
    kv_heads, span = kv_cache.shape[3:5]
    group = heads * tp // kv_heads
    depth, full = out_weight.shape[1:]
    width = full // tp
    vmem = pl.BlockSpec(memory_space=pltpu.VMEM)
    far = list(range(tp))[::-1]

    def everyone(arrays, shift):
        got = {}
        for k in far:
            same = k == 0 and shift == 0
            got[k] = arrays[k] if same else exchanged(arrays[k], k, tp, sections, shift)
        return [got[k] for k in range(tp)]

    all_queries = everyone([queries] * tp, 0)
    moved_residual = exchanged(residual, 0, tp, sections, 1)
    partial = pl.pallas_call(
        functools.partial(attention_kernel, tp, group),
        out_shape=[jax.ShapeDtypeStruct((heads * rows + STAT_ROWS, dim), BF16)] * tp,
        in_specs=[pl.BlockSpec(memory_space=pltpu.SMEM), vmem, vmem] + [vmem] * tp,
        out_specs=[vmem] * tp,
        scratch_shapes=[pltpu.VMEM((heads * tp, rows, span), F32)] * 2,
        compiler_params=params(8),
        name="attention",
    )(lengths, new_kv, kv_cache, *all_queries)
    joined = everyone(partial, 0)
    levels = pl.pallas_call(
        functools.partial(projection_kernel, tp, rows, heads, min(512, width)),
        out_shape=[jax.ShapeDtypeStruct((rows, width), BF16)] * tp,
        in_specs=[pl.BlockSpec(memory_space=pl.ANY)] + [vmem] * tp,
        out_specs=[vmem] * tp,
        scratch_shapes=[pltpu.VMEM((tp, depth, width), BF16), pltpu.SemaphoreType.DMA((tp,))],
        compiler_params=params(40),
        name="projection",
    )(out_weight, *joined)
    got = everyone(levels, 1)
    own = pl.pallas_call(
        functools.partial(sum_kernel, tp),
        out_shape=jax.ShapeDtypeStruct((rows, width), BF16),
        in_specs=[vmem] * (tp + 1),
        out_specs=vmem,
        compiler_params=params(4),
        name="owner_sum",
    )(moved_residual, *got)
    return pl.pallas_call(
        functools.partial(place_kernel, tp),
        out_shape=jax.ShapeDtypeStruct((1, rows, full), BF16),
        in_specs=[vmem] * tp,
        out_specs=vmem,
        compiler_params=params(4),
        name="placed",
    )(*everyone([own] * tp, 0))


def solution(mesh):
    return jax.shard_map(
        functools.partial(local, mesh.shape["tp"], mesh.shape["section"]),
        mesh=mesh,
        in_specs=(
            P("section", "rep", "tp", None),
            P("section", "rep", None, None, None),
            P("section", "rep", None, None, "tp", None),
            P("section", "rep"),
            P("section", "rep", "tp"),
            P("section", "tp", None),
        ),
        out_specs=P("section", "rep", None),
        check_vma=False,
    )
```

```python
import functools
import math

import jax
import jax.numpy as jnp
from jax import lax
from jax.experimental import pallas as pl
from jax.experimental.pallas import tpu as pltpu
from jax.sharding import PartitionSpec as P

QB = 128
LANES = 128
STAT_ROWS = 16
MIB = 1 << 20
F32 = jnp.float32
BF16 = jnp.bfloat16
VMEM_SPEC = pl.BlockSpec(memory_space=pltpu.VMEM)
ANY_SPEC = pl.BlockSpec(memory_space=pl.ANY)


def pieces(x):
    high = x.astype(BF16).astype(F32)
    rest = x - high
    middle = rest.astype(BF16).astype(F32)
    return high, middle, rest - middle


def weight_copies(weight_ref, held_ref, sems, rank, first_slot):
    width = held_ref.shape[2]
    for i in range(held_ref.shape[0]):
        start = pl.multiple_of((rank ^ (2 * i + first_slot)) * width, width)
        yield pltpu.make_async_copy(
            weight_ref.at[0, :, pl.ds(start, width)], held_ref.at[i], sems.at[i]
        )


def stage_cache_kernel(
    lengths_ref, new_ref, kv_ref, weight_ref, held_ref, stored_ref, limit_ref,
    lengths, new, kv, sems, held_sems,
):
    rank = lax.axis_index("tp")
    rows, _, kv_heads, span, dim = kv.shape
    small = [
        pltpu.make_async_copy(lengths_ref, lengths, sems.at[0]),
        pltpu.make_async_copy(new_ref.at[0], new, sems.at[1]),
        pltpu.make_async_copy(kv_ref.at[0], kv, sems.at[2]),
    ]
    held = list(weight_copies(weight_ref, held_ref, held_sems, rank, 1))
    for copy in small + held:
        copy.start()
    for copy in small:
        copy.wait()
    first = rank * span
    sub = lax.broadcasted_iota(jnp.int32, (span, dim), 0)
    row_of = lax.broadcasted_iota(jnp.int32, (rows, span), 0)
    limit = jnp.zeros((rows, span), jnp.int32)
    for r in range(rows):
        limit = jnp.where(row_of == r, lengths[0, r] - first, limit)
        written = sub == lengths[0, r] - first
        for which in range(2):
            fresh = new[r, which].astype(F32)
            for k in range(kv_heads):
                block = kv[r, which, k].astype(F32)
                stored_ref[r, which, k] = jnp.where(written, fresh[k : k + 1], block).astype(BF16)
    limit_ref[...] = limit
    for copy in held:
        copy.wait()


def stage_kernel(weight_ref, after_ref, held_ref, held_sems):
    del after_ref
    rank = lax.axis_index("tp")
    held = list(weight_copies(weight_ref, held_ref, held_sems, rank, 0))
    for copy in held:
        copy.start()
    for copy in held:
        copy.wait()


def attention_kernel(queries_ref, stored_ref, limit_ref, out_ref, scores_ref, mixed_ref):
    tp, rows, heads, dim = queries_ref.shape
    kv_heads, span = stored_ref.shape[2:4]
    group = heads * tp // kv_heads
    per = group // heads
    scale = 1.0 / math.sqrt(dim)

    for m in range(kv_heads):
        for r in range(rows):
            q = jnp.concatenate(
                [queries_ref[m * per + i, r].astype(F32) for i in range(per)], axis=0
            ).astype(BF16)
            s = lax.dot_general(
                q, stored_ref[r, 0, m], (((1,), (1,)), ((), ())), preferred_element_type=F32
            )
            scores_ref[m * group : (m + 1) * group, r, :] = s * scale

    pos = lax.broadcasted_iota(jnp.int32, (rows, span), 1)
    visible = (pos <= limit_ref[...])[None]
    scores = jnp.where(visible, scores_ref[...], -1e30)
    top = jnp.max(scores, axis=-1, keepdims=True)
    weights = jnp.where(visible, jnp.exp(scores - top), 0.0)
    total = jnp.sum(weights, axis=-1, keepdims=True)
    scores_ref[...] = weights

    for m in range(kv_heads):
        for r in range(rows):
            w = scores_ref[m * group : (m + 1) * group, r, :].astype(BF16)
            mixed_ref[m * group : (m + 1) * group, r, :] = jnp.dot(
                w, stored_ref[r, 1, m], preferred_element_type=F32
            )

    n = heads * rows
    sub_n = lax.broadcasted_iota(jnp.int32, (n, LANES), 0)
    lane_n = lax.broadcasted_iota(jnp.int32, (n, LANES), 1)
    stat_sub = lax.broadcasted_iota(jnp.int32, (STAT_ROWS, LANES), 0)
    for j in range(tp):
        own = slice(j * heads, (j + 1) * heads)
        out_ref[j, :n, :] = mixed_ref[own].reshape(n, dim).astype(BF16)
        tops = jnp.where(lane_n == sub_n, top[own].reshape(n, 1), 0.0)
        sums = jnp.where(lane_n == sub_n + n, total[own].reshape(n, 1), 0.0)
        stats = jnp.sum(tops + sums, axis=0, keepdims=True)
        tile = jnp.zeros((STAT_ROWS, LANES), F32)
        for i, piece in enumerate(pieces(stats)):
            tile = jnp.where(stat_sub == i, piece, tile)
        out_ref[j, n:, :] = tile.astype(BF16)


def attended_block(blocks, rows, heads):
    n = rows * heads
    sub_n = lax.broadcasted_iota(jnp.int32, (n, LANES), 0)
    lane_n = lax.broadcasted_iota(jnp.int32, (n, LANES), 1)
    tops, sums = [], []
    for j in range(blocks.shape[0]):
        tile = blocks[j, n:, :].astype(F32)
        stats = tile[0:1] + tile[1:2] + tile[2:3]
        tops.append(jnp.sum(jnp.where(lane_n == sub_n, stats, 0.0), axis=1, keepdims=True))
        sums.append(jnp.sum(jnp.where(lane_n == sub_n + n, stats, 0.0), axis=1, keepdims=True))
    overall = functools.reduce(jnp.maximum, tops)
    total = jnp.zeros((n, 1), F32)
    mixed = jnp.zeros((n, LANES), F32)
    for j, (top, part) in enumerate(zip(tops, sums)):
        factor = jnp.exp(top - overall)
        total = total + part * factor
        mixed = mixed + blocks[j, :n, :].astype(F32) * factor
    attended = mixed / total
    return jnp.concatenate(
        [attended[h * rows : (h + 1) * rows] for h in range(heads)], axis=1
    ).astype(BF16)


def requantized(x):
    top = jnp.max(jnp.abs(x), axis=-1, keepdims=True)
    scale = ((top + 1e-06) / 127.0).astype(BF16).astype(F32)
    return jnp.clip(jnp.floor(x / scale + 0.5), -127.0, 127.0) * scale


def project(flat, held_ref, out_ref):
    slots, _, width = held_ref.shape
    tile = min(512, width)
    for i in range(slots):
        for c in range(0, width, tile):
            part = jnp.dot(flat, held_ref[i, :, c : c + tile], preferred_element_type=F32)
            for b in range(0, tile, QB):
                block = requantized(part[:, b : b + QB])
                out_ref[i, :, c + b : c + b + QB] = block.astype(out_ref.dtype)


def join_project_kernel(rows, heads, blocks_ref, held_ref, after_ref, flat_ref, out_ref):
    del after_ref
    flat = attended_block(blocks_ref, rows, heads)
    flat_ref[...] = flat
    project(flat, held_ref, out_ref)


def project_kernel(flat_ref, held_ref, out_ref):
    project(flat_ref[...], held_ref, out_ref)


def split_kernel(kept_ref, got_ref, send_ref, keep_ref):
    for i in range(send_ref.shape[0]):
        send_ref[i] = (kept_ref[2 * i + 1] + got_ref[2 * i + 1].astype(F32)).astype(BF16)
        keep_ref[i] = kept_ref[2 * i] + got_ref[2 * i].astype(F32)


def total_kernel(kept_ref, got_ref, residual_ref, out_ref):
    own = kept_ref[0] + got_ref[0].astype(F32) + residual_ref[0].astype(F32)
    out_ref[0] = own.astype(BF16)
    out_ref[1] = (kept_ref[1] + got_ref[1].astype(F32)).astype(BF16)


def owner_kernel(near_ref, far_ref, out_ref):
    for i in range(2):
        for b in range(0, out_ref.shape[2], QB):
            at = slice(b, b + QB)
            x = near_ref[i, :, at].astype(F32) + far_ref[1 - i, :, at].astype(F32)
            out_ref[i, :, at] = requantized(x).astype(BF16)


def place_kernel(offsets, high, *refs):
    blocks, out_ref = refs[:-1], refs[-1]
    width = blocks[0].shape[2]
    rank = lax.axis_index("tp")
    for offset, block in zip(offsets, blocks):
        for i in range(2):
            start = pl.multiple_of((rank ^ offset ^ (i * high)) * width, width)
            out_ref[0, :, pl.ds(start, width)] = block[i]


def call(kernel, name, outs, args, in_specs=None, scratch=(), mib=4, cost=MIB):
    return pl.pallas_call(
        kernel,
        out_shape=outs,
        in_specs=in_specs or [VMEM_SPEC] * len(args),
        out_specs=jax.tree.map(lambda _: VMEM_SPEC, outs),
        scratch_shapes=scratch,
        compiler_params=pltpu.CompilerParams(vmem_limit_bytes=mib * MIB),
        cost_estimate=pl.CostEstimate(flops=cost, bytes_accessed=cost, transcendentals=0),
        name=name,
    )(*args)


def in_hbm(array):
    return pltpu.with_memory_space_constraint(array, pltpu.HBM)


def local(tp, sections, queries, new_kv, kv_cache, lengths, residual, out_weight):
    rows, heads, dim = queries.shape[1:]
    kv_heads, span = kv_cache.shape[3:5]
    depth, full = out_weight.shape[1:]
    width = full // tp
    half = tp // 2
    bits = tp.bit_length() - 1
    struct = jax.ShapeDtypeStruct

    def exchanged(array, k, shift=0):
        pairs = [
            (s * tp + t, ((s + shift) % sections) * tp + (t ^ k))
            for s in range(sections)
            for t in range(tp)
        ]
        return lax.ppermute(array, ("section", "tp"), pairs)

    copies = jnp.broadcast_to(queries, (tp, *queries.shape[1:]))
    all_queries = lax.all_to_all(copies, "tp", 0, 0)
    weight = in_hbm(out_weight)
    held_odd, stored, limit = call(
        stage_cache_kernel,
        "stage_cache",
        [
            pltpu.VMEM((half, depth, width), BF16),
            pltpu.VMEM(kv_cache.shape[1:], BF16),
            pltpu.VMEM((rows, span), jnp.int32),
        ],
        (in_hbm(lengths), in_hbm(new_kv), in_hbm(kv_cache), weight),
        in_specs=[ANY_SPEC] * 4,
        scratch=[
            pltpu.SMEM(lengths.shape, jnp.int32),
            pltpu.VMEM(new_kv.shape[1:], BF16),
            pltpu.VMEM(kv_cache.shape[1:], BF16),
            pltpu.SemaphoreType.DMA((3,)),
            pltpu.SemaphoreType.DMA((half,)),
        ],
        cost=18 * MIB,
    )
    partial = call(
        attention_kernel,
        "attention",
        struct((tp, heads * rows + STAT_ROWS, dim), BF16),
        (all_queries, stored, limit),
        scratch=[pltpu.VMEM((heads * tp, rows, span), F32)] * 2,
        cost=8 * MIB,
    )
    joined = lax.all_to_all(partial, "tp", 0, 0)
    held_even = call(
        stage_kernel,
        "stage",
        pltpu.VMEM((half, depth, width), BF16),
        (weight, partial),
        in_specs=[ANY_SPEC] * 2,
        scratch=[pltpu.SemaphoreType.DMA((half,))],
        cost=16 * MIB,
    )
    flat, away = call(
        functools.partial(join_project_kernel, rows, heads),
        "project_away",
        [struct((rows, depth), BF16), struct((half, rows, width), BF16)],
        (joined, held_odd, held_even),
        in_specs=[VMEM_SPEC] * 2 + [ANY_SPEC],
        cost=16 * MIB,
    )
    got = exchanged(away, 1)
    kept = call(
        project_kernel,
        "project_own",
        struct((half, rows, width), F32),
        (flat, held_even),
        cost=16 * MIB,
    )
    for b in range(1, bits - 1):
        slots = kept.shape[0] // 2
        send, kept = call(
            split_kernel,
            "split_sum",
            [struct((slots, rows, width), BF16), struct((slots, rows, width), F32)],
            (kept, got),
        )
        got = exchanged(send, 1 << b)
    high = 1 << (bits - 1)
    total = call(
        total_kernel, "pair_sum", struct((2, rows, width), BF16), (kept, got, residual)
    )
    far = exchanged(total, high, 1)
    near = exchanged(total, 0, 1)
    own = call(owner_kernel, "owner", struct((2, rows, width), BF16), (near, far))
    parts = [(0, own)]
    for b in reversed(range(bits - 1)):
        parts += [(offset ^ (1 << b), exchanged(part, 1 << b)) for offset, part in parts]
    return call(
        functools.partial(place_kernel, [offset for offset, _ in parts], high),
        "placed",
        struct((1, rows, full), BF16),
        [part for _, part in parts],
    )


def solution(mesh):
    return jax.shard_map(
        functools.partial(local, mesh.shape["tp"], mesh.shape["section"]),
        mesh=mesh,
        in_specs=(
            P("section", "rep", "tp", None),
            P("section", "rep", None, None, None),
            P("section", "rep", None, None, "tp", None),
            P("section", "rep"),
            P("section", "rep", "tp"),
            P("section", "tp", None),
        ),
        out_specs=P("section", "rep", None),
        check_vma=False,
    )
```

```python
import functools
import math

import jax
import jax.numpy as jnp
from jax import lax
from jax.experimental import pallas as pl
from jax.experimental.pallas import tpu as pltpu
from jax.sharding import PartitionSpec as P

QB = 128
LANES = 128
STAT_ROWS = 16
MIB = 1 << 20
F32 = jnp.float32
BF16 = jnp.bfloat16
VMEM_SPEC = pl.BlockSpec(memory_space=pltpu.VMEM)
ANY_SPEC = pl.BlockSpec(memory_space=pl.ANY)


def pieces(x):
    high = x.astype(BF16).astype(F32)
    rest = x - high
    middle = rest.astype(BF16).astype(F32)
    return high, middle, rest - middle


def weight_copies(slots, weight_ref, held_ref, sems):
    rank = lax.axis_index("tp")
    width = held_ref.shape[2]
    copies = []
    for i, slot in enumerate(slots):
        start = pl.multiple_of((rank ^ slot) * width, width)
        copies.append(
            pltpu.make_async_copy(
                weight_ref.at[0, :, pl.ds(start, width)], held_ref.at[i], sems.at[i]
            )
        )
    return copies


def stage_cache_kernel(
    per, lengths_ref, new_ref, kv_ref, queries_ref, stored_ref, limit_ref, near_ref,
    lengths, new, kv, sems,
):
    rank = lax.axis_index("tp")
    rows, _, kv_heads, span, dim = kv.shape
    copies = [
        pltpu.make_async_copy(lengths_ref, lengths, sems.at[0]),
        pltpu.make_async_copy(new_ref.at[0], new, sems.at[1]),
        pltpu.make_async_copy(kv_ref.at[0], kv, sems.at[2]),
        pltpu.make_async_copy(queries_ref, near_ref, sems.at[3]),
    ]
    for copy in copies:
        copy.start()
    for copy in copies:
        copy.wait()
    first = rank * span
    sub = lax.broadcasted_iota(jnp.int32, (span, dim), 0)
    kv_sub = lax.broadcasted_iota(jnp.int32, (kv_heads, dim), 0)
    row_of = lax.broadcasted_iota(jnp.int32, (rows, span), 0)
    limit = jnp.zeros((rows, span), jnp.int32)
    for r in range(rows):
        limit = jnp.where(row_of == r, lengths[0, r] - first, limit)
        written = sub == lengths[0, r] - first
        for which in range(2):
            new_heads = new[r, which].astype(F32)
            for m in range(kv_heads):
                head = (rank // per) ^ m
                fresh = jnp.sum(
                    jnp.where(kv_sub == head, new_heads, 0.0), axis=0, keepdims=True
                )
                block = kv[r, which, head].astype(F32)
                stored_ref[r, which, m] = jnp.where(written, fresh, block).astype(BF16)
    limit_ref[...] = limit


def stage_kernel(slots, weight_ref, after_ref, held_ref, sems):
    del after_ref
    copies = weight_copies(slots, weight_ref, held_ref, sems)
    for copy in copies:
        copy.start()
    for copy in copies:
        copy.wait()


def append_kernel(first_ref, second_ref, after_ref, out_ref):
    del after_ref
    count = first_ref.shape[0]
    out_ref[:count] = first_ref[...]
    out_ref[count:] = second_ref[...]


def packed(mixed, top, total):
    stat_sub = lax.broadcasted_iota(jnp.int32, (STAT_ROWS, LANES), 0)
    tile = jnp.zeros((STAT_ROWS, LANES), F32)
    for i, piece in enumerate(pieces(top) + pieces(total)):
        tile = jnp.where(stat_sub == i, piece, tile)
    return jnp.concatenate([mixed, tile], axis=0).astype(BF16)


def to_lanes(column):
    n = column.shape[0]
    sub = lax.broadcasted_iota(jnp.int32, (n, LANES), 0)
    lane = lax.broadcasted_iota(jnp.int32, (n, LANES), 1)
    return jnp.sum(jnp.where(lane == sub, column, 0.0), axis=0, keepdims=True)


def to_column(row, n):
    sub = lax.broadcasted_iota(jnp.int32, (n, LANES), 0)
    lane = lax.broadcasted_iota(jnp.int32, (n, LANES), 1)
    return jnp.sum(jnp.where(lane == sub, row, 0.0), axis=1, keepdims=True)


def merged(first, second):
    n = first.shape[0] - STAT_ROWS
    tops, sums = [], []
    for block in (first, second):
        tile = block[n:].astype(F32)
        tops.append(tile[0:1] + tile[1:2] + tile[2:3])
        sums.append(tile[3:4] + tile[4:5] + tile[5:6])
    top = jnp.maximum(*tops)
    factors = [jnp.exp(own - top) for own in tops]
    total = sums[0] * factors[0] + sums[1] * factors[1]
    mixed = first[:n].astype(F32) * to_column(factors[0], n)
    mixed = mixed + second[:n].astype(F32) * to_column(factors[1], n)
    return mixed, top, total


def attention_kernel(
    low_ref, high_ref, stored_ref, limit_ref, after_ref, send_ref, keep_ref, scores_ref, mixed_ref
):
    del after_ref
    half, rows, heads, dim = low_ref.shape
    tp = 2 * half
    bits = tp.bit_length() - 1
    kv_heads, span = stored_ref.shape[2:4]
    group = heads * tp // kv_heads
    per = group // heads
    scale = 1.0 / math.sqrt(dim)

    def query(k, r):
        source = high_ref if k & 1 else low_ref
        at = sum(((k >> b) & 1) << (bits - 1 - b) for b in range(1, bits))
        return source[at, r].astype(F32)

    for m in range(kv_heads):
        for r in range(rows):
            q = jnp.concatenate([query(m * per + i, r) for i in range(per)], axis=0).astype(BF16)
            s = lax.dot_general(
                q, stored_ref[r, 0, m], (((1,), (1,)), ((), ())), preferred_element_type=F32
            )
            scores_ref[m * group : (m + 1) * group, r, :] = s * scale

    pos = lax.broadcasted_iota(jnp.int32, (rows, span), 1)
    visible = (pos <= limit_ref[...])[None]
    scores = jnp.where(visible, scores_ref[...], -1e30)
    top = jnp.max(scores, axis=-1, keepdims=True)
    weights = jnp.where(visible, jnp.exp(scores - top), 0.0)
    total = jnp.sum(weights, axis=-1, keepdims=True)
    scores_ref[...] = weights

    for m in range(kv_heads):
        for r in range(rows):
            w = scores_ref[m * group : (m + 1) * group, r, :].astype(BF16)
            mixed_ref[m * group : (m + 1) * group, r, :] = jnp.dot(
                w, stored_ref[r, 1, m], preferred_element_type=F32
            )

    n = heads * rows
    for k in range(tp):
        own = slice(k * heads, (k + 1) * heads)
        block = packed(
            mixed_ref[own].reshape(n, dim),
            to_lanes(top[own].reshape(n, 1)),
            to_lanes(total[own].reshape(n, 1)),
        )
        if k & 1:
            send_ref[k >> 1] = block
        else:
            keep_ref[k >> 1] = block


def merge_kernel(kept_ref, got_ref, after_ref, send_ref, keep_ref):
    del after_ref
    for i in range(keep_ref.shape[0]):
        keep_ref[i] = packed(*merged(kept_ref[2 * i], got_ref[2 * i]))
        send_ref[i] = packed(*merged(kept_ref[2 * i + 1], got_ref[2 * i + 1]))


def requantized(x):
    top = jnp.max(jnp.abs(x), axis=-1, keepdims=True)
    scale = ((top + 1e-06) / 127.0).astype(BF16).astype(F32)
    return jnp.clip(jnp.floor(x / scale + 0.5), -127.0, 127.0) * scale


def project_slot(flat, weight, out_ref, i):
    width = weight.shape[1]
    tile = min(512, width)
    for c in range(0, width, tile):
        part = jnp.dot(flat, weight[:, c : c + tile], preferred_element_type=F32)
        for b in range(0, tile, QB):
            block = requantized(part[:, b : b + QB])
            out_ref[i, :, c + b : c + b + QB] = block.astype(out_ref.dtype)


def project_away_kernel(
    rows, heads, places, slots, kept_ref, got_ref, weight_ref, *refs
):
    held, (flat_ref, out_ref, next_ref, sems) = refs[:-4], refs[-4:]
    copies = weight_copies(slots, weight_ref, next_ref, sems)
    for copy in copies:
        copy.start()
    mixed, _, total = merged(kept_ref[0], got_ref[0])
    attended = mixed / to_column(total, mixed.shape[0])
    flat = jnp.concatenate(
        [attended[h * rows : (h + 1) * rows] for h in range(heads)], axis=1
    ).astype(BF16)
    flat_ref[...] = flat
    for i, (array, index) in enumerate(places):
        project_slot(flat, held[array].at[index], out_ref, i)
    for copy in copies:
        copy.wait()


def project_own_kernel(places, slots, order, flat_ref, weight_ref, *refs):
    held, (out_ref, late_ref, sems) = refs[:-3], refs[-3:]
    copies = weight_copies(slots, weight_ref, late_ref, sems)
    for copy in copies:
        copy.start()
    flat = flat_ref[...]
    for i in order:
        if places[i] is None:
            continue
        array, index = places[i]
        project_slot(flat, held[array].at[index], out_ref, i)
    for late, slot in enumerate(slots):
        copies[late].wait()
        project_slot(flat, late_ref.at[late], out_ref, slot >> 1)


def split_kernel(kept_ref, got_ref, send_ref, keep_ref):
    for i in range(send_ref.shape[0]):
        send_ref[i] = (kept_ref[2 * i + 1] + got_ref[2 * i + 1].astype(F32)).astype(BF16)
        keep_ref[i] = kept_ref[2 * i] + got_ref[2 * i].astype(F32)


def total_kernel(kept_ref, got_ref, residual_ref, out_ref):
    own = kept_ref[0] + got_ref[0].astype(F32) + residual_ref[0].astype(F32)
    out_ref[0] = own.astype(BF16)
    out_ref[1] = (kept_ref[1] + got_ref[1].astype(F32)).astype(BF16)


def owner_kernel(near_ref, far_ref, out_ref):
    for i in range(2):
        for b in range(0, out_ref.shape[2], QB):
            at = slice(b, b + QB)
            x = near_ref[i, :, at].astype(F32) + far_ref[1 - i, :, at].astype(F32)
            out_ref[i, :, at] = requantized(x).astype(BF16)


def place_kernel(offsets, high, *refs):
    blocks, out_ref = refs[:-1], refs[-1]
    width = blocks[0].shape[2]
    rank = lax.axis_index("tp")
    for offset, block in zip(offsets, blocks):
        for i in range(2):
            start = pl.multiple_of((rank ^ offset ^ (i * high)) * width, width)
            out_ref[0, :, pl.ds(start, width)] = block[i]


def call(kernel, name, outs, args, in_specs=None, scratch=(), mib=4, cost=MIB):
    return pl.pallas_call(
        kernel,
        out_shape=outs,
        in_specs=in_specs or [VMEM_SPEC] * len(args),
        out_specs=jax.tree.map(lambda _: VMEM_SPEC, outs),
        scratch_shapes=scratch,
        compiler_params=pltpu.CompilerParams(vmem_limit_bytes=mib * MIB),
        cost_estimate=pl.CostEstimate(flops=cost, bytes_accessed=cost, transcendentals=0),
        name=name,
    )(*args)


def in_hbm(array):
    return pltpu.with_memory_space_constraint(array, pltpu.HBM)


def local(tp, sections, queries, new_kv, kv_cache, lengths, residual, out_weight):
    rows, heads, dim = queries.shape[1:]
    kv_heads, span = kv_cache.shape[3:5]
    depth, full = out_weight.shape[1:]
    width = full // tp
    half = tp // 2
    bits = tp.bit_length() - 1
    struct = jax.ShapeDtypeStruct

    def exchanged(array, k, shift=0):
        pairs = [
            (s * tp + t, ((s + shift) % sections) * tp + (t ^ k))
            for s in range(sections)
            for t in range(tp)
        ]
        return lax.ppermute(array, ("section", "tp"), pairs)

    weight = in_hbm(out_weight)
    order = list(range(1, tp, 2)) + list(range(0, tp, 2))
    windows = 2 * bits - 1
    each = max(1, tp * 5 // 8 // windows)
    staged = []

    def stage(after):
        slots = order[len(staged) * each : (len(staged) + 1) * each]
        held = call(
            functools.partial(stage_kernel, slots),
            "stage",
            pltpu.VMEM((each, depth, width), BF16),
            (weight, after),
            in_specs=[ANY_SPEC, VMEM_SPEC],
            scratch=[pltpu.SemaphoreType.DMA((each,))],
            cost=4 * MIB,
        )
        staged.append((slots, held))
        return held

    got = exchanged(queries, 1 << (bits - 1))
    stored, limit, have = call(
        functools.partial(stage_cache_kernel, tp // kv_heads),
        "stage_cache",
        [
            pltpu.VMEM(kv_cache.shape[1:], BF16),
            pltpu.VMEM((rows, span), jnp.int32),
            pltpu.VMEM(queries.shape, BF16),
        ],
        (in_hbm(lengths), in_hbm(new_kv), in_hbm(kv_cache), in_hbm(queries)),
        in_specs=[ANY_SPEC] * 4,
        scratch=[
            pltpu.SMEM(lengths.shape, jnp.int32),
            pltpu.VMEM(new_kv.shape[1:], BF16),
            pltpu.VMEM(kv_cache.shape[1:], BF16),
            pltpu.SemaphoreType.DMA((4,)),
        ],
        cost=4 * MIB,
    )
    after = limit
    for b in reversed(range(bits - 1)):
        count = 2 * have.shape[0]
        have = call(
            append_kernel, "append", struct((count, rows, heads, dim), BF16), (have, got, after)
        )
        got = exchanged(have, 1 << b)
        after = stage(have)
    packed_block = (heads * rows + STAT_ROWS, dim)
    send, kept = call(
        attention_kernel,
        "attention",
        [struct((half, *packed_block), BF16)] * 2,
        (have, got, stored, limit, after),
        scratch=[pltpu.VMEM((heads * tp, rows, span), F32)] * 2,
        cost=8 * MIB,
    )
    got = exchanged(send, 1)
    after = stage(send)
    for b in range(1, bits):
        count = kept.shape[0] // 2
        send, kept = call(
            merge_kernel, "merge", [struct((count, *packed_block), BF16)] * 2, (kept, got, after)
        )
        got = exchanged(send, 1 << b)
        after = stage(send)

    where = {
        slot: (array, i) for array, (slots, _) in enumerate(staged) for i, slot in enumerate(slots)
    }
    rest = order[windows * each :]
    soon, late = rest[: tp // 8], rest[tp // 8 :]
    flat, away, held = call(
        functools.partial(
            project_away_kernel, rows, heads, [where[slot] for slot in range(1, tp, 2)], soon
        ),
        "project_away",
        [
            struct((rows, depth), BF16),
            struct((half, rows, width), BF16),
            pltpu.VMEM((len(soon), depth, width), BF16),
        ],
        (kept, got, weight, *[held for _, held in staged]),
        in_specs=[VMEM_SPEC] * 2 + [ANY_SPEC] + [VMEM_SPEC] * len(staged),
        scratch=[pltpu.SemaphoreType.DMA((len(soon),))],
        cost=16 * MIB,
    )
    got = exchanged(away, 1)
    staged.append((soon, held))
    where.update({slot: (len(staged) - 1, i) for i, slot in enumerate(soon)})
    kept = call(
        functools.partial(
            project_own_kernel,
            [where.get(slot) for slot in range(0, tp, 2)],
            late,
            list(range(half)),
        ),
        "project_own",
        struct((half, rows, width), F32),
        (flat, weight, *[held for _, held in staged]),
        in_specs=[VMEM_SPEC, ANY_SPEC] + [VMEM_SPEC] * len(staged),
        scratch=[
            pltpu.VMEM((len(late), depth, width), BF16),
            pltpu.SemaphoreType.DMA((len(late),)),
        ],
        mib=14,
        cost=16 * MIB,
    )
    for b in range(1, bits - 1):
        slots = kept.shape[0] // 2
        send, kept = call(
            split_kernel,
            "split_sum",
            [struct((slots, rows, width), BF16), struct((slots, rows, width), F32)],
            (kept, got),
        )
        got = exchanged(send, 1 << b)
    high = 1 << (bits - 1)
    total = call(
        total_kernel, "pair_sum", struct((2, rows, width), BF16), (kept, got, residual)
    )
    far = exchanged(total, high, 1)
    near = exchanged(total, 0, 1)
    own = call(owner_kernel, "owner", struct((2, rows, width), BF16), (near, far))
    parts = [(0, own)]
    for b in reversed(range(bits - 1)):
        parts += [(offset ^ (1 << b), exchanged(part, 1 << b)) for offset, part in parts]
    return call(
        functools.partial(place_kernel, [offset for offset, _ in parts], high),
        "placed",
        struct((1, rows, full), BF16),
        [part for _, part in parts],
    )


def solution(mesh):
    return jax.shard_map(
        functools.partial(local, mesh.shape["tp"], mesh.shape["section"]),
        mesh=mesh,
        in_specs=(
            P("section", "rep", "tp", None),
            P("section", "rep", None, None, None),
            P("section", "rep", None, None, "tp", None),
            P("section", "rep"),
            P("section", "rep", "tp"),
            P("section", "tp", None),
        ),
        out_specs=P("section", "rep", None),
        check_vma=False,
    )
```

```python
import functools
import math

import jax
import jax.numpy as jnp
from jax import lax
from jax.experimental import pallas as pl
from jax.experimental.pallas import tpu as pltpu
from jax.sharding import PartitionSpec as P

QB = 128
LANES = 128
STAT_ROWS = 16
MIB = 1 << 20
F32 = jnp.float32
BF16 = jnp.bfloat16
VMEM_SPEC = pl.BlockSpec(memory_space=pltpu.VMEM)
ANY_SPEC = pl.BlockSpec(memory_space=pl.ANY)


def pieces(x):
    high = x.astype(BF16).astype(F32)
    rest = x - high
    middle = rest.astype(BF16).astype(F32)
    return high, middle, rest - middle


def weight_copies(slots, weight_ref, held_ref, sems, cuts=1):
    rank = lax.axis_index("tp")
    width = held_ref.shape[2]
    piece = width // cuts
    copies = []
    for i, slot in enumerate(slots):
        for c in range(cuts):
            start = pl.multiple_of((rank ^ slot) * width + c * piece, piece)
            copies.append(
                pltpu.make_async_copy(
                    weight_ref.at[0, :, pl.ds(start, piece)],
                    held_ref.at[i, :, c * piece : (c + 1) * piece],
                    sems.at[i * cuts + c],
                )
            )
    return copies


def stage_cache_kernel(
    per, slots, lengths_ref, new_ref, kv_ref, queries_ref, weight_ref,
    stored_ref, limit_ref, near_ref, held_ref, lengths, new, kv, sems, held_sems,
):
    rank = lax.axis_index("tp")
    rows, _, kv_heads, span, dim = kv.shape
    copies = [
        pltpu.make_async_copy(lengths_ref, lengths, sems.at[0]),
        pltpu.make_async_copy(new_ref.at[0], new, sems.at[1]),
        pltpu.make_async_copy(kv_ref.at[0], kv, sems.at[2]),
        pltpu.make_async_copy(queries_ref, near_ref, sems.at[3]),
    ]
    held = weight_copies(slots, weight_ref, held_ref, held_sems)
    for copy in copies + held:
        copy.start()
    for copy in copies:
        copy.wait()
    first = rank * span
    sub = lax.broadcasted_iota(jnp.int32, (span, dim), 0)
    kv_sub = lax.broadcasted_iota(jnp.int32, (kv_heads, dim), 0)
    row_of = lax.broadcasted_iota(jnp.int32, (rows, span), 0)
    limit = jnp.zeros((rows, span), jnp.int32)
    for r in range(rows):
        limit = jnp.where(row_of == r, lengths[0, r] - first, limit)
        written = sub == lengths[0, r] - first
        for which in range(2):
            new_heads = new[r, which].astype(F32)
            for m in range(kv_heads):
                head = (rank // per) ^ m
                fresh = jnp.sum(
                    jnp.where(kv_sub == head, new_heads, 0.0), axis=0, keepdims=True
                )
                block = kv[r, which, head].astype(F32)
                stored_ref[r, which, m] = jnp.where(written, fresh, block).astype(BF16)
    limit_ref[...] = limit
    for copy in held:
        copy.wait()


def stage_kernel(slots, weight_ref, after_ref, held_ref, sems):
    del after_ref
    copies = weight_copies(slots, weight_ref, held_ref, sems)
    for copy in copies:
        copy.start()
    for copy in copies:
        copy.wait()


def append_kernel(first_ref, second_ref, after_ref, out_ref):
    del after_ref
    count = first_ref.shape[0]
    out_ref[:count] = first_ref[...]
    out_ref[count:] = second_ref[...]


def packed(mixed, top, total):
    stat_sub = lax.broadcasted_iota(jnp.int32, (STAT_ROWS, LANES), 0)
    tile = jnp.zeros((STAT_ROWS, LANES), F32)
    for i, piece in enumerate(pieces(top) + pieces(total)):
        tile = jnp.where(stat_sub == i, piece, tile)
    return jnp.concatenate([mixed, tile], axis=0).astype(BF16)


def to_lanes(column):
    n = column.shape[0]
    sub = lax.broadcasted_iota(jnp.int32, (n, LANES), 0)
    lane = lax.broadcasted_iota(jnp.int32, (n, LANES), 1)
    return jnp.sum(jnp.where(lane == sub, column, 0.0), axis=0, keepdims=True)


def to_column(row, n):
    sub = lax.broadcasted_iota(jnp.int32, (n, LANES), 0)
    lane = lax.broadcasted_iota(jnp.int32, (n, LANES), 1)
    return jnp.sum(jnp.where(lane == sub, row, 0.0), axis=1, keepdims=True)


def merged(blocks):
    n = blocks[0].shape[0] - STAT_ROWS
    tops, sums = [], []
    for block in blocks:
        tile = block[n:].astype(F32)
        tops.append(tile[0:1] + tile[1:2] + tile[2:3])
        sums.append(tile[3:4] + tile[4:5] + tile[5:6])
    top = functools.reduce(jnp.maximum, tops)
    mixed, total = 0.0, 0.0
    for block, own_top, own_sum in zip(blocks, tops, sums):
        factor = jnp.exp(own_top - top)
        total = total + own_sum * factor
        mixed = mixed + block[:n].astype(F32) * to_column(factor, n)
    return mixed, top, total


def attention_kernel(stored_ref, limit_ref, after_ref, *refs):
    del after_ref
    sources, outs, (scores_ref, mixed_ref) = refs[:4], refs[4:8], refs[8:]
    quarter, rows, heads, dim = sources[0].shape
    tp = 4 * quarter
    kv_heads, span = stored_ref.shape[2:4]
    group = heads * tp // kv_heads
    per = group // heads
    scale = 1.0 / math.sqrt(dim)

    def query(k, r):
        return sources[k // quarter][k % quarter, r].astype(F32)

    for m in range(kv_heads):
        for r in range(rows):
            q = jnp.concatenate([query(m * per + i, r) for i in range(per)], axis=0).astype(BF16)
            s = lax.dot_general(
                q, stored_ref[r, 0, m], (((1,), (1,)), ((), ())), preferred_element_type=F32
            )
            scores_ref[m * group : (m + 1) * group, r, :] = s * scale

    pos = lax.broadcasted_iota(jnp.int32, (rows, span), 1)
    visible = (pos <= limit_ref[...])[None]
    scores = jnp.where(visible, scores_ref[...], -1e30)
    top = jnp.max(scores, axis=-1, keepdims=True)
    weights = jnp.where(visible, jnp.exp(scores - top), 0.0)
    total = jnp.sum(weights, axis=-1, keepdims=True)
    scores_ref[...] = weights

    for m in range(kv_heads):
        for r in range(rows):
            w = scores_ref[m * group : (m + 1) * group, r, :].astype(BF16)
            mixed_ref[m * group : (m + 1) * group, r, :] = jnp.dot(
                w, stored_ref[r, 1, m], preferred_element_type=F32
            )

    n = heads * rows
    for k in range(tp):
        own = slice(k * heads, (k + 1) * heads)
        outs[k // quarter][k % quarter] = packed(
            mixed_ref[own].reshape(n, dim),
            to_lanes(top[own].reshape(n, 1)),
            to_lanes(total[own].reshape(n, 1)),
        )


def merge_kernel(after_ref, *refs):
    del after_ref
    sources, (send_ref, keep_ref) = refs[:-2], refs[-2:]
    count = keep_ref.shape[0]
    for i in range(2 * count):
        block = packed(*merged([source[i] for source in sources]))
        if i < count:
            keep_ref[i] = block
        else:
            send_ref[i - count] = block


def requantized(x):
    top = jnp.max(jnp.abs(x), axis=-1, keepdims=True)
    scale = ((top + 1e-06) / 127.0).astype(BF16).astype(F32)
    return jnp.clip(jnp.floor(x / scale + 0.5), -127.0, 127.0) * scale


def project_columns(flat, weight, out_ref, i, start):
    columns = weight.shape[1]
    tile = min(512, columns)
    for c in range(0, columns, tile):
        part = jnp.dot(flat, weight[:, c : c + tile], preferred_element_type=F32)
        for b in range(0, tile, QB):
            at = start + c + b
            block = requantized(part[:, b : b + QB])
            out_ref[i, :, at : at + QB] = block.astype(out_ref.dtype)


def project_away_kernel(rows, heads, places, kept_ref, got_ref, *refs):
    held, (flat_ref, out_ref) = refs[:-2], refs[-2:]
    mixed, _, total = merged([kept_ref[0], got_ref[0]])
    attended = mixed / to_column(total, mixed.shape[0])
    flat = jnp.concatenate(
        [attended[h * rows : (h + 1) * rows] for h in range(heads)], axis=1
    ).astype(BF16)
    flat_ref[...] = flat
    for i, (array, index) in enumerate(places):
        project_columns(flat, held[array].at[index], out_ref, i, 0)


def project_own_kernel(places, slots, cuts, flat_ref, weight_ref, *refs):
    held, (out_ref, late_ref, sems) = refs[:-3], refs[-3:]
    copies = weight_copies(slots, weight_ref, late_ref, sems, cuts)
    for copy in copies:
        copy.start()
    flat = flat_ref[...]
    for i, place in enumerate(places):
        if place is not None:
            project_columns(flat, held[place[0]].at[place[1]], out_ref, i, 0)
    piece = late_ref.shape[2] // cuts
    for late, slot in enumerate(slots):
        for c in range(cuts):
            copies[late * cuts + c].wait()
            columns = late_ref.at[late, :, c * piece : (c + 1) * piece]
            project_columns(flat, columns, out_ref, slot >> 1, c * piece)


def split_kernel(kept_ref, got_ref, send_ref, keep_ref):
    for i in range(send_ref.shape[0]):
        send_ref[i] = (kept_ref[2 * i + 1] + got_ref[2 * i + 1].astype(F32)).astype(BF16)
        keep_ref[i] = kept_ref[2 * i] + got_ref[2 * i].astype(F32)


def pair_kernel(kept_ref, got_ref, residual_ref, even_ref, odd_ref):
    for i in range(4):
        x = kept_ref[i] + got_ref[i].astype(F32)
        if i == 0:
            x = x + residual_ref[0].astype(F32)
        if i & 1:
            odd_ref[i >> 1] = x.astype(BF16)
        else:
            even_ref[i >> 1] = x.astype(BF16)


def owner_kernel(near_ref, one_ref, two_ref, three_ref, out_ref):
    for i in range(2):
        for b in range(0, out_ref.shape[2], QB):
            at = slice(b, b + QB)
            x = near_ref[i, :, at].astype(F32) + one_ref[i, :, at].astype(F32)
            y = two_ref[1 - i, :, at].astype(F32) + three_ref[1 - i, :, at].astype(F32)
            out_ref[i, :, at] = requantized(x + y).astype(BF16)


def place_kernel(offsets, high, *refs):
    blocks, out_ref = refs[:-1], refs[-1]
    width = blocks[0].shape[2]
    rank = lax.axis_index("tp")
    for offset, block in zip(offsets, blocks):
        for i in range(2):
            start = pl.multiple_of((rank ^ offset ^ (i * high)) * width, width)
            out_ref[0, :, pl.ds(start, width)] = block[i]


def call(kernel, name, outs, args, in_specs=None, scratch=(), mib=4, cost=MIB):
    return pl.pallas_call(
        kernel,
        out_shape=outs,
        in_specs=in_specs or [VMEM_SPEC] * len(args),
        out_specs=jax.tree.map(lambda _: VMEM_SPEC, outs),
        scratch_shapes=scratch,
        compiler_params=pltpu.CompilerParams(vmem_limit_bytes=mib * MIB),
        cost_estimate=pl.CostEstimate(flops=cost, bytes_accessed=cost, transcendentals=0),
        name=name,
    )(*args)


def in_hbm(array):
    return pltpu.with_memory_space_constraint(array, pltpu.HBM)


def local(tp, sections, queries, new_kv, kv_cache, lengths, residual, out_weight):
    rows, heads, dim = queries.shape[1:]
    kv_heads, span = kv_cache.shape[3:5]
    depth, full = out_weight.shape[1:]
    width = full // tp
    half = tp // 2
    bits = tp.bit_length() - 1
    struct = jax.ShapeDtypeStruct

    def exchanged(array, k, shift=0):
        pairs = [
            (s * tp + t, ((s + shift) % sections) * tp + (t ^ k))
            for s in range(sections)
            for t in range(tp)
        ]
        return lax.ppermute(array, ("section", "tp"), pairs)

    weight = in_hbm(out_weight)
    quarter = tp // 4
    groups = [g * quarter for g in range(1, 4)]
    order = list(range(1, tp, 2)) + list(range(0, tp, 2))
    each = tp // 8
    staged = []

    def next_slots(count):
        used = sum(len(slots) for slots, _ in staged)
        return order[used : used + count * each]

    def stage(after, count):
        slots = next_slots(count)
        held = call(
            functools.partial(stage_kernel, slots),
            "stage",
            pltpu.VMEM((len(slots), depth, width), BF16),
            (weight, after),
            in_specs=[ANY_SPEC, VMEM_SPEC],
            scratch=[pltpu.SemaphoreType.DMA((len(slots),))],
            cost=4 * MIB * count,
        )
        staged.append((slots, held))
        return held

    got = exchanged(queries, 1)
    slots = next_slots(1)
    stored, limit, have, held = call(
        functools.partial(stage_cache_kernel, tp // kv_heads, slots),
        "stage_cache",
        [
            pltpu.VMEM(kv_cache.shape[1:], BF16),
            pltpu.VMEM((rows, span), jnp.int32),
            pltpu.VMEM(queries.shape, BF16),
            pltpu.VMEM((len(slots), depth, width), BF16),
        ],
        (in_hbm(lengths), in_hbm(new_kv), in_hbm(kv_cache), in_hbm(queries), weight),
        in_specs=[ANY_SPEC] * 5,
        scratch=[
            pltpu.SMEM(lengths.shape, jnp.int32),
            pltpu.VMEM(new_kv.shape[1:], BF16),
            pltpu.VMEM(kv_cache.shape[1:], BF16),
            pltpu.SemaphoreType.DMA((4,)),
            pltpu.SemaphoreType.DMA((len(slots),)),
        ],
        cost=8 * MIB,
    )
    staged.append((slots, held))
    after = limit
    for b in range(bits - 2):
        count = 2 << b
        have = call(
            append_kernel, "append", struct((count, rows, heads, dim), BF16), (have, got, after)
        )
        after = have
        if b < bits - 3:
            got = exchanged(have, 2 << b)
    all_queries = [have, *(exchanged(have, k) for k in reversed(groups))]
    all_queries[1:] = all_queries[:0:-1]
    after = stage(have, 2)
    packed_block = (heads * rows + STAT_ROWS, dim)
    partial = call(
        attention_kernel,
        "attention",
        [struct((quarter, *packed_block), BF16)] * 4,
        (stored, limit, after, *all_queries),
        scratch=[pltpu.VMEM((heads * tp, rows, span), F32)] * 2,
        cost=8 * MIB,
    )
    pending = [partial[0], *(exchanged(partial[g], g * quarter) for g in (3, 2, 1))]
    after = stage(partial[3], 2)
    for b in reversed(range(bits - 2)):
        send, kept = call(
            merge_kernel, "merge", [struct((1 << b, *packed_block), BF16)] * 2, (after, *pending)
        )
        pending = [kept, exchanged(send, 1 << b)]
        after = send
    stage(send, 1)

    where = {
        slot: (array, i) for array, (slots, _) in enumerate(staged) for i, slot in enumerate(slots)
    }
    late = next_slots(tp)
    held = [array for _, array in staged]
    cuts = max(1, width // 512)
    flat, away = call(
        functools.partial(
            project_away_kernel, rows, heads, [where[slot] for slot in range(1, tp, 2)]
        ),
        "project_away",
        [struct((rows, depth), BF16), struct((half, rows, width), BF16)],
        (*pending, *held),
        cost=16 * MIB,
    )
    got = exchanged(away, 1)
    kept = call(
        functools.partial(
            project_own_kernel, [where.get(slot) for slot in range(0, tp, 2)], late, cuts
        ),
        "project_own",
        struct((half, rows, width), F32),
        (flat, weight, *held),
        in_specs=[VMEM_SPEC, ANY_SPEC] + [VMEM_SPEC] * len(held),
        scratch=[
            pltpu.VMEM((len(late), depth, width), BF16),
            pltpu.SemaphoreType.DMA((len(late) * cuts,)),
        ],
        mib=14,
        cost=16 * MIB,
    )
    for b in range(1, bits - 2):
        slots = kept.shape[0] // 2
        send, kept = call(
            split_kernel,
            "split_sum",
            [struct((slots, rows, width), BF16), struct((slots, rows, width), F32)],
            (kept, got),
        )
        got = exchanged(send, 1 << b)
    even, odd = call(
        pair_kernel, "pair_sum", [struct((2, rows, width), BF16)] * 2, (kept, got, residual)
    )
    three = exchanged(odd, groups[2], 1)
    two = exchanged(even, groups[1], 1)
    one = exchanged(odd, groups[0], 1)
    near = exchanged(even, 0, 1)
    own = call(
        owner_kernel, "owner", struct((2, rows, width), BF16), (near, one, two, three)
    )
    high = 1 << (bits - 1)
    parts = [(0, own)] + [(k, exchanged(own, k)) for k in reversed(range(1, high))]
    return call(
        functools.partial(place_kernel, [offset for offset, _ in parts], high),
        "placed",
        struct((1, rows, full), BF16),
        [part for _, part in parts],
    )


def solution(mesh):
    return jax.shard_map(
        functools.partial(local, mesh.shape["tp"], mesh.shape["section"]),
        mesh=mesh,
        in_specs=(
            P("section", "rep", "tp", None),
            P("section", "rep", None, None, None),
            P("section", "rep", None, None, "tp", None),
            P("section", "rep"),
            P("section", "rep", "tp"),
            P("section", "tp", None),
        ),
        out_specs=P("section", "rep", None),
        check_vma=False,
    )
```

```python
import functools
import math

import jax
import jax.numpy as jnp
from jax import lax
from jax.experimental import pallas as pl
from jax.experimental.pallas import tpu as pltpu
from jax.sharding import PartitionSpec as P

QB = 128
LANES = 128
STAT_ROWS = 16
MIB = 1 << 20
F32 = jnp.float32
BF16 = jnp.bfloat16
VMEM_SPEC = pl.BlockSpec(memory_space=pltpu.VMEM)
ANY_SPEC = pl.BlockSpec(memory_space=pl.ANY)


def pieces(x):
    high = x.astype(BF16).astype(F32)
    rest = x - high
    middle = rest.astype(BF16).astype(F32)
    return high, middle, rest - middle


def weight_copies(units, weight_ref, held_ref, sems):
    rank = lax.axis_index("tp")
    columns = held_ref.shape[2]
    copies = []
    for i, (slot, half) in enumerate(units):
        start = pl.multiple_of(((rank ^ slot) * 2 + half) * columns, columns)
        copies.append(
            pltpu.make_async_copy(
                weight_ref.at[0, :, pl.ds(start, columns)], held_ref.at[i], sems.at[i]
            )
        )
    return copies


def stage_cache_kernel(
    per, units, lengths_ref, new_ref, kv_ref, queries_ref, weight_ref,
    stored_ref, limit_ref, near_ref, held_ref, lengths, new, kv, sems, held_sems,
):
    rank = lax.axis_index("tp")
    rows, _, kv_heads, span, dim = kv.shape
    copies = [
        pltpu.make_async_copy(lengths_ref, lengths, sems.at[0]),
        pltpu.make_async_copy(new_ref.at[0], new, sems.at[1]),
        pltpu.make_async_copy(kv_ref.at[0], kv, sems.at[2]),
        pltpu.make_async_copy(queries_ref, near_ref, sems.at[3]),
    ]
    held = weight_copies(units, weight_ref, held_ref, held_sems)
    for copy in copies + held:
        copy.start()
    for copy in copies:
        copy.wait()
    first = rank * span
    sub = lax.broadcasted_iota(jnp.int32, (span, dim), 0)
    kv_sub = lax.broadcasted_iota(jnp.int32, (kv_heads, dim), 0)
    row_of = lax.broadcasted_iota(jnp.int32, (rows, span), 0)
    limit = jnp.zeros((rows, span), jnp.int32)
    for r in range(rows):
        limit = jnp.where(row_of == r, lengths[0, r] - first, limit)
        written = sub == lengths[0, r] - first
        for which in range(2):
            new_heads = new[r, which].astype(F32)
            for m in range(kv_heads):
                head = (rank // per) ^ m
                fresh = jnp.sum(
                    jnp.where(kv_sub == head, new_heads, 0.0), axis=0, keepdims=True
                )
                block = kv[r, which, head].astype(F32)
                stored_ref[r, which, m] = jnp.where(written, fresh, block).astype(BF16)
    limit_ref[...] = limit
    for copy in held:
        copy.wait()


def stage_kernel(units, weight_ref, after_ref, held_ref, sems):
    del after_ref
    copies = weight_copies(units, weight_ref, held_ref, sems)
    for copy in copies:
        copy.start()
    for copy in copies:
        copy.wait()


def append_kernel(first_ref, second_ref, after_ref, out_ref):
    del after_ref
    count = first_ref.shape[0]
    out_ref[:count] = first_ref[...]
    out_ref[count:] = second_ref[...]


def packed(mixed, top, total):
    stat_sub = lax.broadcasted_iota(jnp.int32, (STAT_ROWS, LANES), 0)
    tile = jnp.zeros((STAT_ROWS, LANES), F32)
    for i, piece in enumerate(pieces(top) + pieces(total)):
        tile = jnp.where(stat_sub == i, piece, tile)
    return jnp.concatenate([mixed, tile], axis=0).astype(BF16)


def to_lanes(column):
    n = column.shape[0]
    sub = lax.broadcasted_iota(jnp.int32, (n, LANES), 0)
    lane = lax.broadcasted_iota(jnp.int32, (n, LANES), 1)
    return jnp.sum(jnp.where(lane == sub, column, 0.0), axis=0, keepdims=True)


def to_column(row, n):
    sub = lax.broadcasted_iota(jnp.int32, (n, LANES), 0)
    lane = lax.broadcasted_iota(jnp.int32, (n, LANES), 1)
    return jnp.sum(jnp.where(lane == sub, row, 0.0), axis=1, keepdims=True)


def merged(blocks):
    n = blocks[0].shape[0] - STAT_ROWS
    tops, sums = [], []
    for block in blocks:
        tile = block[n:].astype(F32)
        tops.append(tile[0:1] + tile[1:2] + tile[2:3])
        sums.append(tile[3:4] + tile[4:5] + tile[5:6])
    top = functools.reduce(jnp.maximum, tops)
    mixed, total = 0.0, 0.0
    for block, own_top, own_sum in zip(blocks, tops, sums):
        factor = jnp.exp(own_top - top)
        total = total + own_sum * factor
        mixed = mixed + block[:n].astype(F32) * to_column(factor, n)
    return mixed, top, total


def attention_kernel(stored_ref, limit_ref, after_ref, *refs):
    del after_ref
    sources, outs, (scores_ref, mixed_ref) = refs[:4], refs[4:8], refs[8:]
    quarter, rows, heads, dim = sources[0].shape
    tp = 4 * quarter
    kv_heads, span = stored_ref.shape[2:4]
    group = heads * tp // kv_heads
    per = group // heads
    scale = 1.0 / math.sqrt(dim)

    def query(k, r):
        return sources[k // quarter][k % quarter, r].astype(F32)

    for m in range(kv_heads):
        for r in range(rows):
            q = jnp.concatenate([query(m * per + i, r) for i in range(per)], axis=0).astype(BF16)
            s = lax.dot_general(
                q, stored_ref[r, 0, m], (((1,), (1,)), ((), ())), preferred_element_type=F32
            )
            scores_ref[m * group : (m + 1) * group, r, :] = s * scale

    pos = lax.broadcasted_iota(jnp.int32, (rows, span), 1)
    visible = (pos <= limit_ref[...])[None]
    scores = jnp.where(visible, scores_ref[...], -1e30)
    top = jnp.max(scores, axis=-1, keepdims=True)
    weights = jnp.where(visible, jnp.exp(scores - top), 0.0)
    total = jnp.sum(weights, axis=-1, keepdims=True)
    scores_ref[...] = weights

    for m in range(kv_heads):
        for r in range(rows):
            w = scores_ref[m * group : (m + 1) * group, r, :].astype(BF16)
            mixed_ref[m * group : (m + 1) * group, r, :] = jnp.dot(
                w, stored_ref[r, 1, m], preferred_element_type=F32
            )

    n = heads * rows
    for k in range(tp):
        own = slice(k * heads, (k + 1) * heads)
        outs[k // quarter][k % quarter] = packed(
            mixed_ref[own].reshape(n, dim),
            to_lanes(top[own].reshape(n, 1)),
            to_lanes(total[own].reshape(n, 1)),
        )


def merge_kernel(after_ref, *refs):
    del after_ref
    sources, (send_ref, keep_ref) = refs[:-2], refs[-2:]
    count = keep_ref.shape[0]
    for i in range(2 * count):
        block = packed(*merged([source[i] for source in sources]))
        if i < count:
            keep_ref[i] = block
        else:
            send_ref[i - count] = block


def requantized(x):
    top = jnp.max(jnp.abs(x), axis=-1, keepdims=True)
    scale = ((top + 1e-06) / 127.0).astype(BF16).astype(F32)
    return jnp.clip(jnp.floor(x / scale + 0.5), -127.0, 127.0) * scale


def project_columns(flat, weight, out_ref, i, start):
    columns = weight.shape[1]
    tile = min(512, columns)
    for c in range(0, columns, tile):
        part = jnp.dot(flat, weight[:, c : c + tile], preferred_element_type=F32)
        for b in range(0, tile, QB):
            at = start + c + b
            block = requantized(part[:, b : b + QB])
            out_ref[i, :, at : at + QB] = block.astype(out_ref.dtype)


def project_units(flat, held, places, out_ref):
    for i, (array, index) in enumerate(places):
        columns = held[array].shape[2]
        project_columns(flat, held[array].at[index], out_ref, i // 2, i % 2 * columns)


def project_away_kernel(rows, heads, places, kept_ref, got_ref, *refs):
    held, (flat_ref, out_ref) = refs[:-2], refs[-2:]
    mixed, _, total = merged([kept_ref[0], got_ref[0]])
    attended = mixed / to_column(total, mixed.shape[0])
    flat = jnp.concatenate(
        [attended[h * rows : (h + 1) * rows] for h in range(heads)], axis=1
    ).astype(BF16)
    flat_ref[...] = flat
    project_units(flat, held, places, out_ref)


def project_own_kernel(places, flat_ref, *refs):
    project_units(flat_ref[...], refs[:-1], places, refs[-1])


def split_kernel(kept_ref, got_ref, send_ref, keep_ref):
    for i in range(send_ref.shape[0]):
        send_ref[i] = (kept_ref[2 * i + 1] + got_ref[2 * i + 1].astype(F32)).astype(BF16)
        keep_ref[i] = kept_ref[2 * i] + got_ref[2 * i].astype(F32)


def pair_kernel(kept_ref, got_ref, residual_ref, even_ref, odd_ref):
    for i in range(4):
        x = kept_ref[i] + got_ref[i].astype(F32)
        if i == 0:
            x = x + residual_ref[0].astype(F32)
        if i & 1:
            odd_ref[i >> 1] = x.astype(BF16)
        else:
            even_ref[i >> 1] = x.astype(BF16)


def owner_kernel(near_ref, one_ref, two_ref, three_ref, out_ref):
    for i in range(2):
        for b in range(0, out_ref.shape[2], QB):
            at = slice(b, b + QB)
            x = near_ref[i, :, at].astype(F32) + one_ref[i, :, at].astype(F32)
            y = two_ref[1 - i, :, at].astype(F32) + three_ref[1 - i, :, at].astype(F32)
            out_ref[i, :, at] = requantized(x + y).astype(BF16)


def place_kernel(offsets, high, *refs):
    blocks, out_ref = refs[:-1], refs[-1]
    width = blocks[0].shape[2]
    rank = lax.axis_index("tp")
    for offset, block in zip(offsets, blocks):
        for i in range(2):
            start = pl.multiple_of((rank ^ offset ^ (i * high)) * width, width)
            out_ref[0, :, pl.ds(start, width)] = block[i]


def call(kernel, name, outs, args, in_specs=None, scratch=(), mib=4, cost=MIB):
    return pl.pallas_call(
        kernel,
        out_shape=outs,
        in_specs=in_specs or [VMEM_SPEC] * len(args),
        out_specs=jax.tree.map(lambda _: VMEM_SPEC, outs),
        scratch_shapes=scratch,
        compiler_params=pltpu.CompilerParams(vmem_limit_bytes=mib * MIB),
        cost_estimate=pl.CostEstimate(flops=cost, bytes_accessed=cost, transcendentals=0),
        name=name,
    )(*args)


def in_hbm(array):
    return pltpu.with_memory_space_constraint(array, pltpu.HBM)


def local(tp, sections, queries, new_kv, kv_cache, lengths, residual, out_weight):
    rows, heads, dim = queries.shape[1:]
    kv_heads, span = kv_cache.shape[3:5]
    depth, full = out_weight.shape[1:]
    width = full // tp
    half = tp // 2
    bits = tp.bit_length() - 1
    struct = jax.ShapeDtypeStruct

    def exchanged(array, k, shift=0):
        pairs = [
            (s * tp + t, ((s + shift) % sections) * tp + (t ^ k))
            for s in range(sections)
            for t in range(tp)
        ]
        return lax.ppermute(array, ("section", "tp"), pairs)

    weight = in_hbm(out_weight)
    quarter = tp // 4
    groups = [g * quarter for g in range(1, 4)]
    order = [(slot, h) for slot in (*range(1, tp, 2), *range(0, tp, 2)) for h in range(2)]
    each = tp // 8
    staged = []

    def next_units(count):
        used = sum(len(units) for units, _ in staged)
        return order[used : used + count * each]

    def held_shape(units):
        return pltpu.VMEM((len(units), depth, width // 2), BF16)

    def stage(after, count):
        units = next_units(count)
        held = call(
            functools.partial(stage_kernel, units),
            "stage",
            held_shape(units),
            (weight, after),
            in_specs=[ANY_SPEC, VMEM_SPEC],
            scratch=[pltpu.SemaphoreType.DMA((len(units),))],
            cost=2 * MIB * count,
        )
        staged.append((units, held))
        return held

    got = exchanged(queries, 1)
    units = next_units(2)
    stored, limit, have, held = call(
        functools.partial(stage_cache_kernel, tp // kv_heads, units),
        "stage_cache",
        [
            pltpu.VMEM(kv_cache.shape[1:], BF16),
            pltpu.VMEM((rows, span), jnp.int32),
            pltpu.VMEM(queries.shape, BF16),
            held_shape(units),
        ],
        (in_hbm(lengths), in_hbm(new_kv), in_hbm(kv_cache), in_hbm(queries), weight),
        in_specs=[ANY_SPEC] * 5,
        scratch=[
            pltpu.SMEM(lengths.shape, jnp.int32),
            pltpu.VMEM(new_kv.shape[1:], BF16),
            pltpu.VMEM(kv_cache.shape[1:], BF16),
            pltpu.SemaphoreType.DMA((4,)),
            pltpu.SemaphoreType.DMA((len(units),)),
        ],
        cost=8 * MIB,
    )
    staged.append((units, held))
    after = limit
    for b in range(bits - 2):
        count = 2 << b
        have = call(
            append_kernel, "append", struct((count, rows, heads, dim), BF16), (have, got, after)
        )
        after = have
        if b < bits - 3:
            got = exchanged(have, 2 << b)
    all_queries = [have, *(exchanged(have, k) for k in reversed(groups))]
    all_queries[1:] = all_queries[:0:-1]
    after = stage(have, 5)
    packed_block = (heads * rows + STAT_ROWS, dim)
    partial = call(
        attention_kernel,
        "attention",
        [struct((quarter, *packed_block), BF16)] * 4,
        (stored, limit, after, *all_queries),
        scratch=[pltpu.VMEM((heads * tp, rows, span), F32)] * 2,
        cost=8 * MIB,
    )
    pending = [partial[0], *(exchanged(partial[g], g * quarter) for g in (1, 2, 3))]
    after = stage(partial[3], 6)
    for b in reversed(range(bits - 2)):
        send, kept = call(
            merge_kernel, "merge", [struct((1 << b, *packed_block), BF16)] * 2, (after, *pending)
        )
        pending = [kept, exchanged(send, 1 << b)]
        after = send
    stage(send, 3)

    where = {
        unit: (array, i) for array, (units, _) in enumerate(staged) for i, unit in enumerate(units)
    }
    places = [where[unit] for unit in order]
    held = [array for _, array in staged]
    flat, away = call(
        functools.partial(project_away_kernel, rows, heads, places[:tp]),
        "project_away",
        [struct((rows, depth), BF16), struct((half, rows, width), BF16)],
        (*pending, *held),
        cost=16 * MIB,
    )
    got = exchanged(away, 1)
    kept = call(
        functools.partial(project_own_kernel, places[tp:]),
        "project_own",
        struct((half, rows, width), F32),
        (flat, *held),
        cost=16 * MIB,
    )
    for b in range(1, bits - 2):
        slots = kept.shape[0] // 2
        send, kept = call(
            split_kernel,
            "split_sum",
            [struct((slots, rows, width), BF16), struct((slots, rows, width), F32)],
            (kept, got),
        )
        got = exchanged(send, 1 << b)
    even, odd = call(
        pair_kernel, "pair_sum", [struct((2, rows, width), BF16)] * 2, (kept, got, residual)
    )
    three = exchanged(odd, groups[2], 1)
    two = exchanged(even, groups[1], 1)
    one = exchanged(odd, groups[0], 1)
    near = exchanged(even, 0, 1)
    own = call(
        owner_kernel, "owner", struct((2, rows, width), BF16), (near, one, two, three)
    )
    high = 1 << (bits - 1)
    parts = [(0, own)] + [(k, exchanged(own, k)) for k in range(1, high)]
    return call(
        functools.partial(place_kernel, [offset for offset, _ in parts], high),
        "placed",
        struct((1, rows, full), BF16),
        [part for _, part in parts],
    )


def solution(mesh):
    return jax.shard_map(
        functools.partial(local, mesh.shape["tp"], mesh.shape["section"]),
        mesh=mesh,
        in_specs=(
            P("section", "rep", "tp", None),
            P("section", "rep", None, None, None),
            P("section", "rep", None, None, "tp", None),
            P("section", "rep"),
            P("section", "rep", "tp"),
            P("section", "tp", None),
        ),
        out_specs=P("section", "rep", None),
        check_vma=False,
    )
```

```python
import functools
import math

import jax
import jax.numpy as jnp
from jax import lax
from jax.experimental import pallas as pl
from jax.experimental.pallas import tpu as pltpu
from jax.sharding import PartitionSpec as P

QB = 128
LANES = 128
STAT_ROWS = 16
MIB = 1 << 20
F32 = jnp.float32
BF16 = jnp.bfloat16
VMEM_SPEC = pl.BlockSpec(memory_space=pltpu.VMEM)
ANY_SPEC = pl.BlockSpec(memory_space=pl.ANY)


def pieces(x):
    high = x.astype(BF16).astype(F32)
    rest = x - high
    middle = rest.astype(BF16).astype(F32)
    return high, middle, rest - middle


def weight_copies(units, weight_ref, held_ref, sems):
    rank = lax.axis_index("tp")
    columns = held_ref.shape[2]
    copies = []
    for i, (slot, half) in enumerate(units):
        start = pl.multiple_of(((rank ^ slot) * 2 + half) * columns, columns)
        copies.append(
            pltpu.make_async_copy(
                weight_ref.at[0, :, pl.ds(start, columns)], held_ref.at[i], sems.at[i]
            )
        )
    return copies


def stage_cache_kernel(
    per, units, lengths_ref, new_ref, kv_ref, queries_ref, weight_ref,
    stored_ref, limit_ref, near_ref, held_ref, lengths, new, kv, sems, held_sems,
):
    rank = lax.axis_index("tp")
    rows, _, kv_heads, span, dim = kv.shape
    copies = [
        pltpu.make_async_copy(lengths_ref, lengths, sems.at[0]),
        pltpu.make_async_copy(new_ref.at[0], new, sems.at[1]),
        pltpu.make_async_copy(kv_ref.at[0], kv, sems.at[2]),
        pltpu.make_async_copy(queries_ref, near_ref, sems.at[3]),
    ]
    held = weight_copies(units, weight_ref, held_ref, held_sems)
    for copy in copies + held:
        copy.start()
    for copy in copies:
        copy.wait()
    first = rank * span
    sub = lax.broadcasted_iota(jnp.int32, (span, dim), 0)
    kv_sub = lax.broadcasted_iota(jnp.int32, (kv_heads, dim), 0)
    row_of = lax.broadcasted_iota(jnp.int32, (rows, span), 0)
    limit = jnp.zeros((rows, span), jnp.int32)
    for r in range(rows):
        limit = jnp.where(row_of == r, lengths[0, r] - first, limit)
        written = sub == lengths[0, r] - first
        for which in range(2):
            new_heads = new[r, which].astype(F32)
            for m in range(kv_heads):
                head = (rank // per) ^ m
                fresh = jnp.sum(
                    jnp.where(kv_sub == head, new_heads, 0.0), axis=0, keepdims=True
                )
                block = kv[r, which, head].astype(F32)
                stored_ref[r, which, m] = jnp.where(written, fresh, block).astype(BF16)
    limit_ref[...] = limit
    for copy in held:
        copy.wait()


def stage_kernel(units, weight_ref, after_ref, held_ref, sems):
    del after_ref
    copies = weight_copies(units, weight_ref, held_ref, sems)
    for copy in copies:
        copy.start()
    for copy in copies:
        copy.wait()


def append_kernel(after_ref, *refs):
    del after_ref
    parts, out_ref = refs[:-1], refs[-1]
    at = 0
    for part in parts:
        out_ref[at : at + part.shape[0]] = part[...]
        at += part.shape[0]


def packed(mixed, top, total):
    stat_sub = lax.broadcasted_iota(jnp.int32, (STAT_ROWS, LANES), 0)
    tile = jnp.zeros((STAT_ROWS, LANES), F32)
    for i, piece in enumerate(pieces(top) + pieces(total)):
        tile = jnp.where(stat_sub == i, piece, tile)
    return jnp.concatenate([mixed, tile], axis=0).astype(BF16)


def to_lanes(column):
    n = column.shape[0]
    sub = lax.broadcasted_iota(jnp.int32, (n, LANES), 0)
    lane = lax.broadcasted_iota(jnp.int32, (n, LANES), 1)
    return jnp.sum(jnp.where(lane == sub, column, 0.0), axis=0, keepdims=True)


def to_column(row, n):
    sub = lax.broadcasted_iota(jnp.int32, (n, LANES), 0)
    lane = lax.broadcasted_iota(jnp.int32, (n, LANES), 1)
    return jnp.sum(jnp.where(lane == sub, row, 0.0), axis=1, keepdims=True)


def merged(blocks):
    n = blocks[0].shape[0] - STAT_ROWS
    tops, sums = [], []
    for block in blocks:
        tile = block[n:].astype(F32)
        tops.append(tile[0:1] + tile[1:2] + tile[2:3])
        sums.append(tile[3:4] + tile[4:5] + tile[5:6])
    top = functools.reduce(jnp.maximum, tops)
    mixed, total = 0.0, 0.0
    for block, own_top, own_sum in zip(blocks, tops, sums):
        factor = jnp.exp(own_top - top)
        total = total + own_sum * factor
        mixed = mixed + block[:n].astype(F32) * to_column(factor, n)
    return mixed, top, total


def place(k, tp):
    quarter = tp // 4
    at = k % quarter * 4 + k // quarter
    return at // (tp // 2), at % (tp // 2)


def attention_kernel(stored_ref, limit_ref, after_ref, *refs):
    del after_ref
    sources, outs, (scores_ref, mixed_ref) = refs[:2], refs[2:4], refs[4:]
    half, rows, heads, dim = sources[0].shape
    tp = 2 * half
    kv_heads, span = stored_ref.shape[2:4]
    group = heads * tp // kv_heads
    per = group // heads
    scale = 1.0 / math.sqrt(dim)

    def query(k, r):
        array, at = place(k, tp)
        return sources[array][at, r].astype(F32)

    for m in range(kv_heads):
        for r in range(rows):
            q = jnp.concatenate([query(m * per + i, r) for i in range(per)], axis=0).astype(BF16)
            s = lax.dot_general(
                q, stored_ref[r, 0, m], (((1,), (1,)), ((), ())), preferred_element_type=F32
            )
            scores_ref[m * group : (m + 1) * group, r, :] = s * scale

    pos = lax.broadcasted_iota(jnp.int32, (rows, span), 1)
    visible = (pos <= limit_ref[...])[None]
    scores = jnp.where(visible, scores_ref[...], -1e30)
    top = jnp.max(scores, axis=-1, keepdims=True)
    weights = jnp.where(visible, jnp.exp(scores - top), 0.0)
    total = jnp.sum(weights, axis=-1, keepdims=True)
    scores_ref[...] = weights

    for m in range(kv_heads):
        for r in range(rows):
            w = scores_ref[m * group : (m + 1) * group, r, :].astype(BF16)
            mixed_ref[m * group : (m + 1) * group, r, :] = jnp.dot(
                w, stored_ref[r, 1, m], preferred_element_type=F32
            )

    n = heads * rows
    for k in range(tp):
        own = slice(k * heads, (k + 1) * heads)
        array, at = place(k, tp)
        outs[array][at] = packed(
            mixed_ref[own].reshape(n, dim),
            to_lanes(top[own].reshape(n, 1)),
            to_lanes(total[own].reshape(n, 1)),
        )


def merge_kernel(after_ref, kept_ref, got_ref, *out_refs):
    del after_ref
    at = 0
    for out_ref in out_refs:
        for i in range(out_ref.shape[0]):
            out_ref[i] = packed(*merged([kept_ref[at], got_ref[at]]))
            at += 1


def requantized(x):
    top = jnp.max(jnp.abs(x), axis=-1, keepdims=True)
    scale = ((top + 1e-06) / 127.0).astype(BF16).astype(F32)
    return jnp.clip(jnp.floor(x / scale + 0.5), -127.0, 127.0) * scale


def project_columns(flat, weight, out_ref, i, start):
    columns = weight.shape[1]
    tile = min(512, columns)
    for c in range(0, columns, tile):
        part = jnp.dot(flat, weight[:, c : c + tile], preferred_element_type=F32)
        for b in range(0, tile, QB):
            at = start + c + b
            block = requantized(part[:, b : b + QB])
            out_ref[i, :, at : at + QB] = block.astype(out_ref.dtype)


def project_units(flat, held, places, out_ref):
    for i, (array, index) in enumerate(places):
        columns = held[array].shape[2]
        project_columns(flat, held[array].at[index], out_ref, i // 2, i % 2 * columns)


def project_away_kernel(rows, heads, places, *refs):
    sources, held, (flat_ref, out_ref) = refs[:4], refs[4:-2], refs[-2:]
    mixed, _, total = merged([source[0] for source in sources])
    attended = mixed / to_column(total, mixed.shape[0])
    flat = jnp.concatenate(
        [attended[h * rows : (h + 1) * rows] for h in range(heads)], axis=1
    ).astype(BF16)
    flat_ref[...] = flat
    project_units(flat, held, places, out_ref)


def project_own_kernel(places, units, flat_ref, weight_ref, *refs):
    held, (out_ref, late_ref, sems) = refs[:-3], refs[-3:]
    copies = weight_copies(units, weight_ref, late_ref, sems)
    for copy in copies:
        copy.start()
    flat = flat_ref[...]
    project_units(flat, held, places, out_ref)
    columns = late_ref.shape[2]
    for i, copy in enumerate(copies, len(places)):
        copy.wait()
        late = late_ref.at[i - len(places)]
        project_columns(flat, late, out_ref, i // 2, i % 2 * columns)


def split_kernel(kept_ref, got_ref, send_ref, keep_ref):
    for i in range(send_ref.shape[0]):
        send_ref[i] = (kept_ref[2 * i + 1] + got_ref[2 * i + 1].astype(F32)).astype(BF16)
        keep_ref[i] = kept_ref[2 * i] + got_ref[2 * i].astype(F32)


def pair_kernel(kept_ref, got_ref, residual_ref, even_ref, odd_ref):
    for i in range(4):
        x = kept_ref[i] + got_ref[i].astype(F32)
        if i == 0:
            x = x + residual_ref[0].astype(F32)
        if i & 1:
            odd_ref[i >> 1] = x.astype(BF16)
        else:
            even_ref[i >> 1] = x.astype(BF16)


def owner_kernel(near_ref, one_ref, two_ref, three_ref, out_ref):
    for i in range(2):
        for b in range(0, out_ref.shape[2], QB):
            at = slice(b, b + QB)
            x = near_ref[i, :, at].astype(F32) + one_ref[i, :, at].astype(F32)
            y = two_ref[1 - i, :, at].astype(F32) + three_ref[1 - i, :, at].astype(F32)
            out_ref[i, :, at] = requantized(x + y).astype(BF16)


def place_kernel(offsets, high, *refs):
    blocks, out_ref = refs[:-1], refs[-1]
    width = blocks[0].shape[2]
    rank = lax.axis_index("tp")
    for offset, block in zip(offsets, blocks):
        for i in range(2):
            start = pl.multiple_of((rank ^ offset ^ (i * high)) * width, width)
            out_ref[0, :, pl.ds(start, width)] = block[i]


def call(kernel, name, outs, args, in_specs=None, scratch=(), mib=4, cost=MIB):
    return pl.pallas_call(
        kernel,
        out_shape=outs,
        in_specs=in_specs or [VMEM_SPEC] * len(args),
        out_specs=jax.tree.map(lambda _: VMEM_SPEC, outs),
        scratch_shapes=scratch,
        compiler_params=pltpu.CompilerParams(vmem_limit_bytes=mib * MIB),
        cost_estimate=pl.CostEstimate(flops=cost, bytes_accessed=cost, transcendentals=0),
        name=name,
    )(*args)


def in_hbm(array):
    return pltpu.with_memory_space_constraint(array, pltpu.HBM)


def local(tp, sections, queries, new_kv, kv_cache, lengths, residual, out_weight):
    rows, heads, dim = queries.shape[1:]
    kv_heads, span = kv_cache.shape[3:5]
    depth, full = out_weight.shape[1:]
    width = full // tp
    half = tp // 2
    bits = tp.bit_length() - 1
    struct = jax.ShapeDtypeStruct

    def exchanged(array, k, shift=0):
        pairs = [
            (s * tp + t, ((s + shift) % sections) * tp + (t ^ k))
            for s in range(sections)
            for t in range(tp)
        ]
        return lax.ppermute(array, ("section", "tp"), pairs)

    weight = in_hbm(out_weight)
    quarter = tp // 4
    groups = [g * quarter for g in range(1, 4)]
    order = [(slot, h) for slot in (*range(1, tp, 2), *range(0, tp, 2)) for h in range(2)]
    each = tp // 8
    staged = []

    def next_units(count):
        used = sum(len(units) for units, _ in staged)
        return order[used : used + count * each]

    def held_shape(units):
        return pltpu.VMEM((len(units), depth, width // 2), BF16)

    def stage(after, count):
        units = next_units(count)
        held = call(
            functools.partial(stage_kernel, units),
            "stage",
            held_shape(units),
            (weight, after),
            in_specs=[ANY_SPEC, VMEM_SPEC],
            scratch=[pltpu.SemaphoreType.DMA((len(units),))],
            cost=2 * MIB * count,
        )
        staged.append((units, held))
        return held

    groups_got = [exchanged(queries, k) for k in reversed(groups)][::-1]
    units = next_units(2)
    stored, limit, have, held = call(
        functools.partial(stage_cache_kernel, tp // kv_heads, units),
        "stage_cache",
        [
            pltpu.VMEM(kv_cache.shape[1:], BF16),
            pltpu.VMEM((rows, span), jnp.int32),
            pltpu.VMEM(queries.shape, BF16),
            held_shape(units),
        ],
        (in_hbm(lengths), in_hbm(new_kv), in_hbm(kv_cache), in_hbm(queries), weight),
        in_specs=[ANY_SPEC] * 5,
        scratch=[
            pltpu.SMEM(lengths.shape, jnp.int32),
            pltpu.VMEM(new_kv.shape[1:], BF16),
            pltpu.VMEM(kv_cache.shape[1:], BF16),
            pltpu.SemaphoreType.DMA((4,)),
            pltpu.SemaphoreType.DMA((len(units),)),
        ],
        cost=8 * MIB,
    )
    staged.append((units, held))
    have, after = [have, *groups_got], limit
    for b in range(bits - 2):
        count = 4 << b
        have = call(
            append_kernel, "append", struct((count, rows, heads, dim), BF16), (after, *have)
        )
        after = have
        have = [have, exchanged(have, 1 << b)]
    after = stage(after, 4)
    packed_block = (heads * rows + STAT_ROWS, dim)
    kept, send = call(
        attention_kernel,
        "attention",
        [struct((half, *packed_block), BF16)] * 2,
        (stored, limit, after, *have),
        scratch=[pltpu.VMEM((heads * tp, rows, span), F32)] * 2,
        cost=8 * MIB,
    )
    got = exchanged(send, quarter // 2)
    after = stage(send, 4)
    for b in reversed(range(bits - 3)):
        kept, send = call(
            merge_kernel, "merge", [struct((4 << b, *packed_block), BF16)] * 2, (after, kept, got)
        )
        got = exchanged(send, 1 << b)
        after = send
    pending = call(
        merge_kernel, "merge", [struct((1, *packed_block), BF16)] * 4, (after, kept, got)
    )
    last = pending[3]
    pending = [pending[0], *(exchanged(block, k) for block, k in zip(pending[1:], groups))]
    stage(last, 3)

    where = {
        unit: (array, i) for array, (units, _) in enumerate(staged) for i, unit in enumerate(units)
    }
    places = [where[unit] for unit in order if unit in where]
    late = order[len(places) :]
    held = [array for _, array in staged]
    flat, away = call(
        functools.partial(project_away_kernel, rows, heads, places[:tp]),
        "project_away",
        [struct((rows, depth), BF16), struct((half, rows, width), BF16)],
        (*pending, *held),
        cost=16 * MIB,
    )
    got = exchanged(away, 1)
    kept = call(
        functools.partial(project_own_kernel, places[tp:], late),
        "project_own",
        struct((half, rows, width), F32),
        (flat, weight, *held),
        in_specs=[VMEM_SPEC, ANY_SPEC] + [VMEM_SPEC] * len(held),
        scratch=[
            pltpu.VMEM((len(late), depth, width // 2), BF16),
            pltpu.SemaphoreType.DMA((len(late),)),
        ],
        mib=14,
        cost=16 * MIB,
    )
    for b in range(1, bits - 2):
        slots = kept.shape[0] // 2
        send, kept = call(
            split_kernel,
            "split_sum",
            [struct((slots, rows, width), BF16), struct((slots, rows, width), F32)],
            (kept, got),
        )
        got = exchanged(send, 1 << b)
    even, odd = call(
        pair_kernel, "pair_sum", [struct((2, rows, width), BF16)] * 2, (kept, got, residual)
    )
    three = exchanged(odd, groups[2], 1)
    two = exchanged(even, groups[1], 1)
    one = exchanged(odd, groups[0], 1)
    near = exchanged(even, 0, 1)
    own = call(
        owner_kernel, "owner", struct((2, rows, width), BF16), (near, one, two, three)
    )
    high = 1 << (bits - 1)
    parts = [(0, own)] + [(k, exchanged(own, k)) for k in range(1, high)]
    return call(
        functools.partial(place_kernel, [offset for offset, _ in parts], high),
        "placed",
        struct((1, rows, full), BF16),
        [part for _, part in parts],
    )


def solution(mesh):
    return jax.shard_map(
        functools.partial(local, mesh.shape["tp"], mesh.shape["section"]),
        mesh=mesh,
        in_specs=(
            P("section", "rep", "tp", None),
            P("section", "rep", None, None, None),
            P("section", "rep", None, None, "tp", None),
            P("section", "rep"),
            P("section", "rep", "tp"),
            P("section", "tp", None),
        ),
        out_specs=P("section", "rep", None),
        check_vma=False,
    )
```

```python
import functools
import math

import jax
import jax.numpy as jnp
from jax import lax
from jax.experimental import pallas as pl
from jax.experimental.pallas import tpu as pltpu
from jax.sharding import PartitionSpec as P

QB = 128
LANES = 128
STAT_ROWS = 16
MIB = 1 << 20
F32 = jnp.float32
BF16 = jnp.bfloat16
VMEM_SPEC = pl.BlockSpec(memory_space=pltpu.VMEM)
ANY_SPEC = pl.BlockSpec(memory_space=pl.ANY)


def pieces(x):
    high = x.astype(BF16).astype(F32)
    rest = x - high
    middle = rest.astype(BF16).astype(F32)
    return high, middle, rest - middle


def weight_copies(units, weight_ref, held_ref, sems):
    rank = lax.axis_index("tp")
    columns = held_ref.shape[2]
    copies = []
    for i, (slot, half) in enumerate(units):
        start = pl.multiple_of(((rank ^ slot) * 2 + half) * columns, columns)
        copies.append(
            pltpu.make_async_copy(
                weight_ref.at[0, :, pl.ds(start, columns)], held_ref.at[i], sems.at[i]
            )
        )
    return copies


def stage_cache_kernel(
    per, units, lengths_ref, new_ref, kv_ref, queries_ref, weight_ref,
    stored_ref, limit_ref, near_ref, held_ref, lengths, new, kv, sems, held_sems,
):
    rank = lax.axis_index("tp")
    rows, _, kv_heads, span, dim = kv.shape
    copies = [
        pltpu.make_async_copy(lengths_ref, lengths, sems.at[0]),
        pltpu.make_async_copy(new_ref.at[0], new, sems.at[1]),
        pltpu.make_async_copy(kv_ref.at[0], kv, sems.at[2]),
        pltpu.make_async_copy(queries_ref, near_ref, sems.at[3]),
    ]
    held = weight_copies(units, weight_ref, held_ref, held_sems)
    for copy in copies + held:
        copy.start()
    for copy in copies:
        copy.wait()
    first = rank * span
    sub = lax.broadcasted_iota(jnp.int32, (span, dim), 0)
    kv_sub = lax.broadcasted_iota(jnp.int32, (kv_heads, dim), 0)
    row_of = lax.broadcasted_iota(jnp.int32, (rows, span), 0)
    limit = jnp.zeros((rows, span), jnp.int32)
    for r in range(rows):
        limit = jnp.where(row_of == r, lengths[0, r] - first, limit)
        written = sub == lengths[0, r] - first
        for which in range(2):
            new_heads = new[r, which].astype(F32)
            for m in range(kv_heads):
                head = (rank // per) ^ m
                fresh = jnp.sum(
                    jnp.where(kv_sub == head, new_heads, 0.0), axis=0, keepdims=True
                )
                block = kv[r, which, head].astype(F32)
                stored_ref[r, which, m] = jnp.where(written, fresh, block).astype(BF16)
    limit_ref[...] = limit
    for copy in held:
        copy.wait()


def stage_kernel(units, weight_ref, after_ref, held_ref, sems):
    del after_ref
    copies = weight_copies(units, weight_ref, held_ref, sems)
    for copy in copies:
        copy.start()
    for copy in copies:
        copy.wait()


def append_kernel(after_ref, *refs):
    del after_ref
    parts, out_ref = refs[:-1], refs[-1]
    at = 0
    for part in parts:
        out_ref[at : at + part.shape[0]] = part[...]
        at += part.shape[0]


def packed(mixed, top, total):
    stat_sub = lax.broadcasted_iota(jnp.int32, (STAT_ROWS, LANES), 0)
    tile = jnp.zeros((STAT_ROWS, LANES), F32)
    for i, piece in enumerate(pieces(top) + pieces(total)):
        tile = jnp.where(stat_sub == i, piece, tile)
    return jnp.concatenate([mixed, tile], axis=0).astype(BF16)


def to_lanes(column):
    n = column.shape[0]
    sub = lax.broadcasted_iota(jnp.int32, (n, LANES), 0)
    lane = lax.broadcasted_iota(jnp.int32, (n, LANES), 1)
    return jnp.sum(jnp.where(lane == sub, column, 0.0), axis=0, keepdims=True)


def to_column(row, n):
    sub = lax.broadcasted_iota(jnp.int32, (n, LANES), 0)
    lane = lax.broadcasted_iota(jnp.int32, (n, LANES), 1)
    return jnp.sum(jnp.where(lane == sub, row, 0.0), axis=1, keepdims=True)


def merged(blocks):
    n = blocks[0].shape[0] - STAT_ROWS
    tops, sums = [], []
    for block in blocks:
        tile = block[n:].astype(F32)
        tops.append(tile[0:1] + tile[1:2] + tile[2:3])
        sums.append(tile[3:4] + tile[4:5] + tile[5:6])
    top = functools.reduce(jnp.maximum, tops)
    mixed, total = 0.0, 0.0
    for block, own_top, own_sum in zip(blocks, tops, sums):
        factor = jnp.exp(own_top - top)
        total = total + own_sum * factor
        mixed = mixed + block[:n].astype(F32) * to_column(factor, n)
    return mixed, top, total


def place(k, tp):
    quarter = tp // 4
    at = k % quarter * 4 + k // quarter
    return at // (tp // 2), at % (tp // 2)


def attention_kernel(stored_ref, limit_ref, after_ref, *refs):
    del after_ref
    sources, outs, (scores_ref, mixed_ref) = refs[:4], refs[4:6], refs[6:]
    quarter, rows, heads, dim = sources[0].shape
    tp = 4 * quarter
    kv_heads, span = stored_ref.shape[2:4]
    group = heads * tp // kv_heads
    per = group // heads
    scale = 1.0 / math.sqrt(dim)

    def query(k, r):
        return sources[k // quarter][k % quarter, r].astype(F32)

    for m in range(kv_heads):
        for r in range(rows):
            q = jnp.concatenate([query(m * per + i, r) for i in range(per)], axis=0).astype(BF16)
            s = lax.dot_general(
                q, stored_ref[r, 0, m], (((1,), (1,)), ((), ())), preferred_element_type=F32
            )
            scores_ref[m * group : (m + 1) * group, r, :] = s * scale

    pos = lax.broadcasted_iota(jnp.int32, (rows, span), 1)
    visible = (pos <= limit_ref[...])[None]
    scores = jnp.where(visible, scores_ref[...], -1e30)
    top = jnp.max(scores, axis=-1, keepdims=True)
    weights = jnp.where(visible, jnp.exp(scores - top), 0.0)
    total = jnp.sum(weights, axis=-1, keepdims=True)
    scores_ref[...] = weights

    for m in range(kv_heads):
        for r in range(rows):
            w = scores_ref[m * group : (m + 1) * group, r, :].astype(BF16)
            mixed_ref[m * group : (m + 1) * group, r, :] = jnp.dot(
                w, stored_ref[r, 1, m], preferred_element_type=F32
            )

    n = heads * rows
    for k in range(tp):
        own = slice(k * heads, (k + 1) * heads)
        array, at = place(k, tp)
        outs[array][at] = packed(
            mixed_ref[own].reshape(n, dim),
            to_lanes(top[own].reshape(n, 1)),
            to_lanes(total[own].reshape(n, 1)),
        )


def merge_kernel(after_ref, kept_ref, got_ref, *out_refs):
    del after_ref
    at = 0
    for out_ref in out_refs:
        for i in range(out_ref.shape[0]):
            out_ref[i] = packed(*merged([kept_ref[at], got_ref[at]]))
            at += 1


def requantized(x):
    top = jnp.max(jnp.abs(x), axis=-1, keepdims=True)
    scale = ((top + 1e-06) / 127.0).astype(BF16).astype(F32)
    return jnp.clip(jnp.floor(x / scale + 0.5), -127.0, 127.0) * scale


def project_columns(flat, weight, out_ref, i, start):
    columns = weight.shape[1]
    tile = min(512, columns)
    for c in range(0, columns, tile):
        part = jnp.dot(flat, weight[:, c : c + tile], preferred_element_type=F32)
        for b in range(0, tile, QB):
            at = start + c + b
            block = requantized(part[:, b : b + QB])
            out_ref[i, :, at : at + QB] = block.astype(out_ref.dtype)


def project_units(flat, held, places, out_ref):
    for i, (array, index) in enumerate(places):
        columns = held[array].shape[2]
        project_columns(flat, held[array].at[index], out_ref, i // 2, i % 2 * columns)


def project_away_kernel(rows, heads, places, *refs):
    sources, held, (flat_ref, out_ref) = refs[:4], refs[4:-2], refs[-2:]
    mixed, _, total = merged([source[0] for source in sources])
    attended = mixed / to_column(total, mixed.shape[0])
    flat = jnp.concatenate(
        [attended[h * rows : (h + 1) * rows] for h in range(heads)], axis=1
    ).astype(BF16)
    flat_ref[...] = flat
    project_units(flat, held, places, out_ref)


def project_own_kernel(places, units, flat_ref, weight_ref, *refs):
    held, (out_ref, late_ref, sems) = refs[:-3], refs[-3:]
    copies = weight_copies(units, weight_ref, late_ref, sems)
    for copy in copies:
        copy.start()
    flat = flat_ref[...]
    project_units(flat, held, places, out_ref)
    columns = late_ref.shape[2]
    for i, copy in enumerate(copies, len(places)):
        copy.wait()
        late = late_ref.at[i - len(places)]
        project_columns(flat, late, out_ref, i // 2, i % 2 * columns)


def split_kernel(kept_ref, got_ref, send_ref, keep_ref):
    for i in range(send_ref.shape[0]):
        send_ref[i] = (kept_ref[2 * i + 1] + got_ref[2 * i + 1].astype(F32)).astype(BF16)
        keep_ref[i] = kept_ref[2 * i] + got_ref[2 * i].astype(F32)


def pair_kernel(kept_ref, got_ref, residual_ref, even_ref, odd_ref):
    for i in range(4):
        x = kept_ref[i] + got_ref[i].astype(F32)
        if i == 0:
            x = x + residual_ref[0].astype(F32)
        if i & 1:
            odd_ref[i >> 1] = x.astype(BF16)
        else:
            even_ref[i >> 1] = x.astype(BF16)


def owner_kernel(near_ref, one_ref, two_ref, three_ref, out_ref):
    for i in range(2):
        for b in range(0, out_ref.shape[2], QB):
            at = slice(b, b + QB)
            x = near_ref[i, :, at].astype(F32) + one_ref[i, :, at].astype(F32)
            y = two_ref[1 - i, :, at].astype(F32) + three_ref[1 - i, :, at].astype(F32)
            out_ref[i, :, at] = requantized(x + y).astype(BF16)


def place_kernel(offsets, high, *refs):
    blocks, out_ref = refs[:-1], refs[-1]
    width = blocks[0].shape[2]
    rank = lax.axis_index("tp")
    for offset, block in zip(offsets, blocks):
        for i in range(2):
            start = pl.multiple_of((rank ^ offset ^ (i * high)) * width, width)
            out_ref[0, :, pl.ds(start, width)] = block[i]


def call(kernel, name, outs, args, in_specs=None, scratch=(), mib=4, cost=MIB):
    return pl.pallas_call(
        kernel,
        out_shape=outs,
        in_specs=in_specs or [VMEM_SPEC] * len(args),
        out_specs=jax.tree.map(lambda _: VMEM_SPEC, outs),
        scratch_shapes=scratch,
        compiler_params=pltpu.CompilerParams(vmem_limit_bytes=mib * MIB),
        cost_estimate=pl.CostEstimate(flops=cost, bytes_accessed=cost, transcendentals=0),
        name=name,
    )(*args)


def in_hbm(array):
    return pltpu.with_memory_space_constraint(array, pltpu.HBM)


def local(tp, sections, queries, new_kv, kv_cache, lengths, residual, out_weight):
    rows, heads, dim = queries.shape[1:]
    kv_heads, span = kv_cache.shape[3:5]
    depth, full = out_weight.shape[1:]
    width = full // tp
    half = tp // 2
    bits = tp.bit_length() - 1
    struct = jax.ShapeDtypeStruct

    def exchanged(array, k, shift=0):
        pairs = [
            (s * tp + t, ((s + shift) % sections) * tp + (t ^ k))
            for s in range(sections)
            for t in range(tp)
        ]
        return lax.ppermute(array, ("section", "tp"), pairs)

    weight = in_hbm(out_weight)
    quarter = tp // 4
    groups = [g * quarter for g in range(1, 4)]
    order = [(slot, h) for slot in (*range(1, tp, 2), *range(0, tp, 2)) for h in range(2)]
    each = tp // 8
    staged = []

    def next_units(count):
        used = sum(len(units) for units, _ in staged)
        return order[used : used + count * each]

    def held_shape(units):
        return pltpu.VMEM((len(units), depth, width // 2), BF16)

    def stage(after, count):
        units = next_units(count)
        held = call(
            functools.partial(stage_kernel, units),
            "stage",
            held_shape(units),
            (weight, after),
            in_specs=[ANY_SPEC, VMEM_SPEC],
            scratch=[pltpu.SemaphoreType.DMA((len(units),))],
            cost=2 * MIB * count,
        )
        staged.append((units, held))
        return held

    got = exchanged(queries, 1)
    units = next_units(2)
    stored, limit, have, held = call(
        functools.partial(stage_cache_kernel, tp // kv_heads, units),
        "stage_cache",
        [
            pltpu.VMEM(kv_cache.shape[1:], BF16),
            pltpu.VMEM((rows, span), jnp.int32),
            pltpu.VMEM(queries.shape, BF16),
            held_shape(units),
        ],
        (in_hbm(lengths), in_hbm(new_kv), in_hbm(kv_cache), in_hbm(queries), weight),
        in_specs=[ANY_SPEC] * 5,
        scratch=[
            pltpu.SMEM(lengths.shape, jnp.int32),
            pltpu.VMEM(new_kv.shape[1:], BF16),
            pltpu.VMEM(kv_cache.shape[1:], BF16),
            pltpu.SemaphoreType.DMA((4,)),
            pltpu.SemaphoreType.DMA((len(units),)),
        ],
        cost=8 * MIB,
    )
    staged.append((units, held))
    after = limit
    for b in range(bits - 2):
        count = 2 << b
        have = call(
            append_kernel, "append", struct((count, rows, heads, dim), BF16), (after, have, got)
        )
        after = have
        if b < bits - 3:
            got = exchanged(have, 2 << b)
    all_queries = [have, *(exchanged(have, k) for k in reversed(groups))]
    all_queries[1:] = all_queries[:0:-1]
    after = stage(have, 5)
    packed_block = (heads * rows + STAT_ROWS, dim)
    kept, send = call(
        attention_kernel,
        "attention",
        [struct((half, *packed_block), BF16)] * 2,
        (stored, limit, after, *all_queries),
        scratch=[pltpu.VMEM((heads * tp, rows, span), F32)] * 2,
        cost=8 * MIB,
    )
    got = exchanged(send, quarter // 2)
    after = stage(send, 4)
    for b in reversed(range(bits - 3)):
        kept, send = call(
            merge_kernel, "merge", [struct((4 << b, *packed_block), BF16)] * 2, (after, kept, got)
        )
        got = exchanged(send, 1 << b)
        after = send
    pending = call(
        merge_kernel, "merge", [struct((1, *packed_block), BF16)] * 4, (after, kept, got)
    )
    last = pending[3]
    pending = [pending[0], *(exchanged(block, k) for block, k in zip(pending[1:], groups))]
    stage(last, 3)

    where = {
        unit: (array, i) for array, (units, _) in enumerate(staged) for i, unit in enumerate(units)
    }
    places = [where[unit] for unit in order if unit in where]
    late = order[len(places) :]
    held = [array for _, array in staged]
    flat, away = call(
        functools.partial(project_away_kernel, rows, heads, places[:tp]),
        "project_away",
        [struct((rows, depth), BF16), struct((half, rows, width), BF16)],
        (*pending, *held),
        cost=16 * MIB,
    )
    got = exchanged(away, 1)
    kept = call(
        functools.partial(project_own_kernel, places[tp:], late),
        "project_own",
        struct((half, rows, width), F32),
        (flat, weight, *held),
        in_specs=[VMEM_SPEC, ANY_SPEC] + [VMEM_SPEC] * len(held),
        scratch=[
            pltpu.VMEM((len(late), depth, width // 2), BF16),
            pltpu.SemaphoreType.DMA((len(late),)),
        ],
        mib=14,
        cost=16 * MIB,
    )
    for b in range(1, bits - 2):
        slots = kept.shape[0] // 2
        send, kept = call(
            split_kernel,
            "split_sum",
            [struct((slots, rows, width), BF16), struct((slots, rows, width), F32)],
            (kept, got),
        )
        got = exchanged(send, 1 << b)
    even, odd = call(
        pair_kernel, "pair_sum", [struct((2, rows, width), BF16)] * 2, (kept, got, residual)
    )
    three = exchanged(odd, groups[2])
    two = exchanged(even, groups[1])
    one = exchanged(odd, groups[0])
    own = call(
        owner_kernel, "owner", struct((2, rows, width), BF16), (even, one, two, three)
    )
    high = 1 << (bits - 1)
    parts = [(k, exchanged(own, k, 1)) for k in range(high)]
    return call(
        functools.partial(place_kernel, [offset for offset, _ in parts], high),
        "placed",
        struct((1, rows, full), BF16),
        [part for _, part in parts],
    )


def solution(mesh):
    return jax.shard_map(
        functools.partial(local, mesh.shape["tp"], mesh.shape["section"]),
        mesh=mesh,
        in_specs=(
            P("section", "rep", "tp", None),
            P("section", "rep", None, None, None),
            P("section", "rep", None, None, "tp", None),
            P("section", "rep"),
            P("section", "rep", "tp"),
            P("section", "tp", None),
        ),
        out_specs=P("section", "rep", None),
        check_vma=False,
    )
```

```python
import functools
import math

import jax
import jax.numpy as jnp
from jax import lax
from jax.experimental import pallas as pl
from jax.experimental.pallas import tpu as pltpu
from jax.sharding import PartitionSpec as P

QB = 128
LANES = 128
STAT_ROWS = 16
MIB = 1 << 20
F32 = jnp.float32
BF16 = jnp.bfloat16
VMEM_SPEC = pl.BlockSpec(memory_space=pltpu.VMEM)
ANY_SPEC = pl.BlockSpec(memory_space=pl.ANY)


def pieces(x):
    high = x.astype(BF16).astype(F32)
    rest = x - high
    middle = rest.astype(BF16).astype(F32)
    return high, middle, rest - middle


def weight_copies(units, weight_ref, held_ref, sems):
    rank = lax.axis_index("tp")
    columns = held_ref.shape[2]
    copies = []
    for i, (slot, half) in enumerate(units):
        start = pl.multiple_of(((rank ^ slot) * 2 + half) * columns, columns)
        copies.append(
            pltpu.make_async_copy(
                weight_ref.at[0, :, pl.ds(start, columns)], held_ref.at[i], sems.at[i]
            )
        )
    return copies


def stage_cache_kernel(
    per, units, lengths_ref, new_ref, kv_ref, queries_ref, weight_ref,
    stored_ref, limit_ref, near_ref, held_ref, lengths, new, kv, sems, held_sems,
):
    rank = lax.axis_index("tp")
    rows, _, kv_heads, span, dim = kv.shape
    copies = [
        pltpu.make_async_copy(lengths_ref, lengths, sems.at[0]),
        pltpu.make_async_copy(new_ref.at[0], new, sems.at[1]),
        pltpu.make_async_copy(kv_ref.at[0], kv, sems.at[2]),
        pltpu.make_async_copy(queries_ref, near_ref, sems.at[3]),
    ]
    held = weight_copies(units, weight_ref, held_ref, held_sems)
    for copy in copies + held:
        copy.start()
    for copy in copies:
        copy.wait()
    first = rank * span
    sub = lax.broadcasted_iota(jnp.int32, (span, dim), 0)
    kv_sub = lax.broadcasted_iota(jnp.int32, (kv_heads, dim), 0)
    row_of = lax.broadcasted_iota(jnp.int32, (rows, span), 0)
    limit = jnp.zeros((rows, span), jnp.int32)
    for r in range(rows):
        limit = jnp.where(row_of == r, lengths[0, r] - first, limit)
        written = sub == lengths[0, r] - first
        for which in range(2):
            new_heads = new[r, which].astype(F32)
            for m in range(kv_heads):
                head = (rank // per) ^ m
                fresh = jnp.sum(
                    jnp.where(kv_sub == head, new_heads, 0.0), axis=0, keepdims=True
                )
                block = kv[r, which, head].astype(F32)
                stored_ref[r, which, m] = jnp.where(written, fresh, block).astype(BF16)
    limit_ref[...] = limit
    for copy in held:
        copy.wait()


def stage_kernel(units, weight_ref, after_ref, held_ref, sems):
    del after_ref
    copies = weight_copies(units, weight_ref, held_ref, sems)
    for copy in copies:
        copy.start()
    for copy in copies:
        copy.wait()


def append_kernel(after_ref, *refs):
    del after_ref
    parts, out_ref = refs[:-1], refs[-1]
    at = 0
    for part in parts:
        out_ref[at : at + part.shape[0]] = part[...]
        at += part.shape[0]


def packed(mixed, top, total):
    stat_sub = lax.broadcasted_iota(jnp.int32, (STAT_ROWS, LANES), 0)
    tile = jnp.zeros((STAT_ROWS, LANES), F32)
    for i, piece in enumerate(pieces(top) + pieces(total)):
        tile = jnp.where(stat_sub == i, piece, tile)
    return jnp.concatenate([mixed, tile], axis=0).astype(BF16)


def to_lanes(column):
    n = column.shape[0]
    sub = lax.broadcasted_iota(jnp.int32, (n, LANES), 0)
    lane = lax.broadcasted_iota(jnp.int32, (n, LANES), 1)
    return jnp.sum(jnp.where(lane == sub, column, 0.0), axis=0, keepdims=True)


def to_column(row, n):
    sub = lax.broadcasted_iota(jnp.int32, (n, LANES), 0)
    lane = lax.broadcasted_iota(jnp.int32, (n, LANES), 1)
    return jnp.sum(jnp.where(lane == sub, row, 0.0), axis=1, keepdims=True)


def merged(blocks):
    n = blocks[0].shape[0] - STAT_ROWS
    tops, sums = [], []
    for block in blocks:
        tile = block[n:].astype(F32)
        tops.append(tile[0:1] + tile[1:2] + tile[2:3])
        sums.append(tile[3:4] + tile[4:5] + tile[5:6])
    top = functools.reduce(jnp.maximum, tops)
    mixed, total = 0.0, 0.0
    for block, own_top, own_sum in zip(blocks, tops, sums):
        factor = jnp.exp(own_top - top)
        total = total + own_sum * factor
        mixed = mixed + block[:n].astype(F32) * to_column(factor, n)
    return mixed, top, total


def place(k, tp):
    quarter = tp // 4
    top = k // quarter
    at = k % quarter * 4 + top % 2 * 2 + top // 2
    return at // (tp // 2), at % (tp // 2)


def attention_kernel(stored_ref, limit_ref, after_ref, *refs):
    del after_ref
    sources, outs, (scores_ref, mixed_ref) = refs[:4], refs[4:6], refs[6:]
    quarter, rows, heads, dim = sources[0].shape
    tp = 4 * quarter
    kv_heads, span = stored_ref.shape[2:4]
    group = heads * tp // kv_heads
    per = group // heads
    scale = 1.0 / math.sqrt(dim)

    def query(k, r):
        return sources[k // quarter][k % quarter, r].astype(F32)

    for m in range(kv_heads):
        for r in range(rows):
            q = jnp.concatenate([query(m * per + i, r) for i in range(per)], axis=0).astype(BF16)
            s = lax.dot_general(
                q, stored_ref[r, 0, m], (((1,), (1,)), ((), ())), preferred_element_type=F32
            )
            scores_ref[m * group : (m + 1) * group, r, :] = s * scale

    pos = lax.broadcasted_iota(jnp.int32, (rows, span), 1)
    visible = (pos <= limit_ref[...])[None]
    scores = jnp.where(visible, scores_ref[...], -1e30)
    top = jnp.max(scores, axis=-1, keepdims=True)
    weights = jnp.where(visible, jnp.exp(scores - top), 0.0)
    total = jnp.sum(weights, axis=-1, keepdims=True)
    scores_ref[...] = weights

    for m in range(kv_heads):
        for r in range(rows):
            w = scores_ref[m * group : (m + 1) * group, r, :].astype(BF16)
            mixed_ref[m * group : (m + 1) * group, r, :] = jnp.dot(
                w, stored_ref[r, 1, m], preferred_element_type=F32
            )

    n = heads * rows
    for k in range(tp):
        own = slice(k * heads, (k + 1) * heads)
        array, at = place(k, tp)
        outs[array][at] = packed(
            mixed_ref[own].reshape(n, dim),
            to_lanes(top[own].reshape(n, 1)),
            to_lanes(total[own].reshape(n, 1)),
        )


def merge_kernel(after_ref, kept_ref, got_ref, *out_refs):
    del after_ref
    at = 0
    for out_ref in out_refs:
        for i in range(out_ref.shape[0]):
            out_ref[i] = packed(*merged([kept_ref[at], got_ref[at]]))
            at += 1


def requantized(x):
    top = jnp.max(jnp.abs(x), axis=-1, keepdims=True)
    scale = ((top + 1e-06) / 127.0).astype(BF16).astype(F32)
    return jnp.clip(jnp.floor(x / scale + 0.5), -127.0, 127.0) * scale


def project_columns(flat, weight, out_ref, i, start):
    columns = weight.shape[1]
    tile = min(512, columns)
    for c in range(0, columns, tile):
        part = jnp.dot(flat, weight[:, c : c + tile], preferred_element_type=F32)
        for b in range(0, tile, QB):
            at = start + c + b
            block = requantized(part[:, b : b + QB])
            out_ref[i, :, at : at + QB] = block.astype(out_ref.dtype)


def project_units(flat, held, places, out_ref):
    for i, (array, index) in enumerate(places):
        columns = held[array].shape[2]
        project_columns(flat, held[array].at[index], out_ref, i // 2, i % 2 * columns)


def project_away_kernel(rows, heads, places, kept_ref, got_ref, *refs):
    held, (flat_ref, out_ref) = refs[:-2], refs[-2:]
    mixed, _, total = merged([kept_ref[0], got_ref[0]])
    attended = mixed / to_column(total, mixed.shape[0])
    flat = jnp.concatenate(
        [attended[h * rows : (h + 1) * rows] for h in range(heads)], axis=1
    ).astype(BF16)
    flat_ref[...] = flat
    project_units(flat, held, places, out_ref)


def project_own_kernel(places, units, flat_ref, weight_ref, *refs):
    held, (out_ref, late_ref, sems) = refs[:-3], refs[-3:]
    copies = weight_copies(units, weight_ref, late_ref, sems)
    for copy in copies:
        copy.start()
    flat = flat_ref[...]
    project_units(flat, held, places, out_ref)
    columns = late_ref.shape[2]
    for i, copy in enumerate(copies, len(places)):
        copy.wait()
        late = late_ref.at[i - len(places)]
        project_columns(flat, late, out_ref, i // 2, i % 2 * columns)


def split_kernel(kept_ref, got_ref, send_ref, keep_ref):
    for i in range(send_ref.shape[0]):
        send_ref[i] = (kept_ref[2 * i + 1] + got_ref[2 * i + 1].astype(F32)).astype(BF16)
        keep_ref[i] = kept_ref[2 * i] + got_ref[2 * i].astype(F32)


def pair_kernel(kept_ref, got_ref, residual_ref, even_ref, odd_ref):
    for i in range(4):
        x = kept_ref[i] + got_ref[i].astype(F32)
        if i == 0:
            x = x + residual_ref[0].astype(F32)
        if i & 1:
            odd_ref[i >> 1] = x.astype(BF16)
        else:
            even_ref[i >> 1] = x.astype(BF16)


def owner_kernel(near_ref, one_ref, two_ref, three_ref, out_ref):
    for i in range(2):
        for b in range(0, out_ref.shape[2], QB):
            at = slice(b, b + QB)
            x = near_ref[i, :, at].astype(F32) + one_ref[i, :, at].astype(F32)
            y = two_ref[1 - i, :, at].astype(F32) + three_ref[1 - i, :, at].astype(F32)
            out_ref[i, :, at] = requantized(x + y).astype(BF16)


def place_kernel(offsets, high, *refs):
    blocks, out_ref = refs[:-1], refs[-1]
    width = blocks[0].shape[2]
    rank = lax.axis_index("tp")
    for offset, block in zip(offsets, blocks):
        for i in range(2):
            start = pl.multiple_of((rank ^ offset ^ (i * high)) * width, width)
            out_ref[0, :, pl.ds(start, width)] = block[i]


def call(kernel, name, outs, args, in_specs=None, scratch=(), mib=4, cost=MIB):
    return pl.pallas_call(
        kernel,
        out_shape=outs,
        in_specs=in_specs or [VMEM_SPEC] * len(args),
        out_specs=jax.tree.map(lambda _: VMEM_SPEC, outs),
        scratch_shapes=scratch,
        compiler_params=pltpu.CompilerParams(vmem_limit_bytes=mib * MIB),
        cost_estimate=pl.CostEstimate(flops=cost, bytes_accessed=cost, transcendentals=0),
        name=name,
    )(*args)


def in_hbm(array):
    return pltpu.with_memory_space_constraint(array, pltpu.HBM)


def local(tp, sections, queries, new_kv, kv_cache, lengths, residual, out_weight):
    rows, heads, dim = queries.shape[1:]
    kv_heads, span = kv_cache.shape[3:5]
    depth, full = out_weight.shape[1:]
    width = full // tp
    half = tp // 2
    bits = tp.bit_length() - 1
    struct = jax.ShapeDtypeStruct

    def exchanged(array, k, shift=0):
        pairs = [
            (s * tp + t, ((s + shift) % sections) * tp + (t ^ k))
            for s in range(sections)
            for t in range(tp)
        ]
        return lax.ppermute(array, ("section", "tp"), pairs)

    weight = in_hbm(out_weight)
    quarter = tp // 4
    groups = [g * quarter for g in range(1, 4)]
    order = [(slot, h) for slot in (*range(1, tp, 2), *range(0, tp, 2)) for h in range(2)]
    each = tp // 8
    staged = []

    def next_units(count):
        used = sum(len(units) for units, _ in staged)
        return order[used : used + count * each]

    def held_shape(units):
        return pltpu.VMEM((len(units), depth, width // 2), BF16)

    def stage(after, count):
        units = next_units(count)
        held = call(
            functools.partial(stage_kernel, units),
            "stage",
            held_shape(units),
            (weight, after),
            in_specs=[ANY_SPEC, VMEM_SPEC],
            scratch=[pltpu.SemaphoreType.DMA((len(units),))],
            cost=2 * MIB * count,
        )
        staged.append((units, held))
        return held

    got = exchanged(queries, 1)
    units = next_units(2)
    stored, limit, have, held = call(
        functools.partial(stage_cache_kernel, tp // kv_heads, units),
        "stage_cache",
        [
            pltpu.VMEM(kv_cache.shape[1:], BF16),
            pltpu.VMEM((rows, span), jnp.int32),
            pltpu.VMEM(queries.shape, BF16),
            held_shape(units),
        ],
        (in_hbm(lengths), in_hbm(new_kv), in_hbm(kv_cache), in_hbm(queries), weight),
        in_specs=[ANY_SPEC] * 5,
        scratch=[
            pltpu.SMEM(lengths.shape, jnp.int32),
            pltpu.VMEM(new_kv.shape[1:], BF16),
            pltpu.VMEM(kv_cache.shape[1:], BF16),
            pltpu.SemaphoreType.DMA((4,)),
            pltpu.SemaphoreType.DMA((len(units),)),
        ],
        cost=8 * MIB,
    )
    staged.append((units, held))
    after = limit
    for b in range(bits - 2):
        count = 2 << b
        have = call(
            append_kernel, "append", struct((count, rows, heads, dim), BF16), (after, have, got)
        )
        after = have
        if b < bits - 3:
            got = exchanged(have, 2 << b)
    all_queries = [have, *(exchanged(have, k) for k in reversed(groups))]
    all_queries[1:] = all_queries[:0:-1]
    after = stage(have, 2)
    packed_block = (heads * rows + STAT_ROWS, dim)
    kept, send = call(
        attention_kernel,
        "attention",
        [struct((half, *packed_block), BF16)] * 2,
        (stored, limit, after, *all_queries),
        scratch=[pltpu.VMEM((heads * tp, rows, span), F32)] * 2,
        cost=8 * MIB,
    )
    got = exchanged(send, quarter // 2)
    after = stage(send, 4)
    count = half
    for k in [1 << b for b in reversed(range(bits - 3))] + groups[:2]:
        count //= 2
        kept, send = call(
            merge_kernel, "merge", [struct((count, *packed_block), BF16)] * 2, (after, kept, got)
        )
        got = exchanged(send, k)
        after = stage(send, 3) if k in groups else send

    where = {
        unit: (array, i) for array, (units, _) in enumerate(staged) for i, unit in enumerate(units)
    }
    places = [where[unit] for unit in order if unit in where]
    late = order[len(places) :]
    held = [array for _, array in staged]
    flat, away = call(
        functools.partial(project_away_kernel, rows, heads, places[:tp]),
        "project_away",
        [struct((rows, depth), BF16), struct((half, rows, width), BF16)],
        (kept, got, *held),
        cost=16 * MIB,
    )
    got = exchanged(away, 1)
    kept = call(
        functools.partial(project_own_kernel, places[tp:], late),
        "project_own",
        struct((half, rows, width), F32),
        (flat, weight, *held),
        in_specs=[VMEM_SPEC, ANY_SPEC] + [VMEM_SPEC] * len(held),
        scratch=[
            pltpu.VMEM((len(late), depth, width // 2), BF16),
            pltpu.SemaphoreType.DMA((len(late),)),
        ],
        mib=14,
        cost=16 * MIB,
    )
    for b in range(1, bits - 2):
        slots = kept.shape[0] // 2
        send, kept = call(
            split_kernel,
            "split_sum",
            [struct((slots, rows, width), BF16), struct((slots, rows, width), F32)],
            (kept, got),
        )
        got = exchanged(send, 1 << b)
    even, odd = call(
        pair_kernel, "pair_sum", [struct((2, rows, width), BF16)] * 2, (kept, got, residual)
    )
    three = exchanged(odd, groups[2])
    two = exchanged(even, groups[1])
    one = exchanged(odd, groups[0])
    own = call(
        owner_kernel, "owner", struct((2, rows, width), BF16), (even, one, two, three)
    )
    high = 1 << (bits - 1)
    parts = [(k, exchanged(own, k, 1)) for k in range(high)]
    return call(
        functools.partial(place_kernel, [offset for offset, _ in parts], high),
        "placed",
        struct((1, rows, full), BF16),
        [part for _, part in parts],
    )


def solution(mesh):
    return jax.shard_map(
        functools.partial(local, mesh.shape["tp"], mesh.shape["section"]),
        mesh=mesh,
        in_specs=(
            P("section", "rep", "tp", None),
            P("section", "rep", None, None, None),
            P("section", "rep", None, None, "tp", None),
            P("section", "rep"),
            P("section", "rep", "tp"),
            P("section", "tp", None),
        ),
        out_specs=P("section", "rep", None),
        check_vma=False,
    )
```

```python
import functools
import math

import jax
import jax.numpy as jnp
from jax import lax
from jax.experimental import pallas as pl
from jax.experimental.pallas import tpu as pltpu
from jax.sharding import PartitionSpec as P

QB = 128
LANES = 128
STAT_ROWS = 16
MIB = 1 << 20
F32 = jnp.float32
BF16 = jnp.bfloat16
VMEM_SPEC = pl.BlockSpec(memory_space=pltpu.VMEM)
ANY_SPEC = pl.BlockSpec(memory_space=pl.ANY)


def pieces(x):
    high = x.astype(BF16).astype(F32)
    rest = x - high
    middle = rest.astype(BF16).astype(F32)
    return high, middle, rest - middle


def weight_copies(units, weight_ref, held_ref, sems):
    rank = lax.axis_index("tp")
    columns = held_ref.shape[2]
    copies = []
    for i, (slot, half) in enumerate(units):
        start = pl.multiple_of(((rank ^ slot) * 2 + half) * columns, columns)
        copies.append(
            pltpu.make_async_copy(
                weight_ref.at[0, :, pl.ds(start, columns)], held_ref.at[i], sems.at[i]
            )
        )
    return copies


def stage_cache_kernel(
    per, units, lengths_ref, new_ref, kv_ref, queries_ref, weight_ref,
    stored_ref, limit_ref, near_ref, held_ref, lengths, new, kv, sems, held_sems,
):
    rank = lax.axis_index("tp")
    rows, _, kv_heads, span, dim = kv.shape
    copies = [
        pltpu.make_async_copy(lengths_ref, lengths, sems.at[0]),
        pltpu.make_async_copy(new_ref.at[0], new, sems.at[1]),
        pltpu.make_async_copy(kv_ref.at[0], kv, sems.at[2]),
        pltpu.make_async_copy(queries_ref, near_ref, sems.at[3]),
    ]
    held = weight_copies(units, weight_ref, held_ref, held_sems)
    for copy in copies + held:
        copy.start()
    for copy in copies:
        copy.wait()
    first = rank * span
    sub = lax.broadcasted_iota(jnp.int32, (span, dim), 0)
    kv_sub = lax.broadcasted_iota(jnp.int32, (kv_heads, dim), 0)
    row_of = lax.broadcasted_iota(jnp.int32, (rows, span), 0)
    limit = jnp.zeros((rows, span), jnp.int32)
    for r in range(rows):
        limit = jnp.where(row_of == r, lengths[0, r] - first, limit)
        written = sub == lengths[0, r] - first
        for which in range(2):
            new_heads = new[r, which].astype(F32)
            for m in range(kv_heads):
                head = (rank // per) ^ m
                fresh = jnp.sum(
                    jnp.where(kv_sub == head, new_heads, 0.0), axis=0, keepdims=True
                )
                block = kv[r, which, head].astype(F32)
                stored_ref[r, which, m] = jnp.where(written, fresh, block).astype(BF16)
    limit_ref[...] = limit
    for copy in held:
        copy.wait()


def stage_kernel(units, weight_ref, after_ref, held_ref, sems):
    del after_ref
    copies = weight_copies(units, weight_ref, held_ref, sems)
    for copy in copies:
        copy.start()
    for copy in copies:
        copy.wait()


def append_kernel(after_ref, *refs):
    del after_ref
    parts, out_ref = refs[:-1], refs[-1]
    at = 0
    for part in parts:
        out_ref[at : at + part.shape[0]] = part[...]
        at += part.shape[0]


def packed(mixed, top, total):
    stat_sub = lax.broadcasted_iota(jnp.int32, (STAT_ROWS, LANES), 0)
    tile = jnp.zeros((STAT_ROWS, LANES), F32)
    for i, piece in enumerate(pieces(top) + pieces(total)):
        tile = jnp.where(stat_sub == i, piece, tile)
    return jnp.concatenate([mixed, tile], axis=0).astype(BF16)


def to_lanes(column):
    n = column.shape[0]
    sub = lax.broadcasted_iota(jnp.int32, (n, LANES), 0)
    lane = lax.broadcasted_iota(jnp.int32, (n, LANES), 1)
    return jnp.sum(jnp.where(lane == sub, column, 0.0), axis=0, keepdims=True)


def to_column(row, n):
    sub = lax.broadcasted_iota(jnp.int32, (n, LANES), 0)
    lane = lax.broadcasted_iota(jnp.int32, (n, LANES), 1)
    return jnp.sum(jnp.where(lane == sub, row, 0.0), axis=1, keepdims=True)


def merged(blocks):
    n = blocks[0].shape[0] - STAT_ROWS
    tops, sums = [], []
    for block in blocks:
        tile = block[n:].astype(F32)
        tops.append(tile[0:1] + tile[1:2] + tile[2:3])
        sums.append(tile[3:4] + tile[4:5] + tile[5:6])
    top = functools.reduce(jnp.maximum, tops)
    mixed, total = 0.0, 0.0
    for block, own_top, own_sum in zip(blocks, tops, sums):
        factor = jnp.exp(own_top - top)
        total = total + own_sum * factor
        mixed = mixed + block[:n].astype(F32) * to_column(factor, n)
    return mixed, top, total


def place(k, tp):
    quarter = tp // 4
    at = k % quarter * 4 + (4 - k // quarter) % 4
    return at // (tp // 2), at % (tp // 2)


def attention_kernel(stored_ref, limit_ref, after_ref, *refs):
    del after_ref
    sources, outs, (scores_ref, mixed_ref) = refs[:4], refs[4:6], refs[6:]
    quarter, rows, heads, dim = sources[0].shape
    tp = 4 * quarter
    kv_heads, span = stored_ref.shape[2:4]
    group = heads * tp // kv_heads
    per = group // heads
    scale = 1.0 / math.sqrt(dim)

    def query(k, r):
        return sources[k // quarter][k % quarter, r].astype(F32)

    for m in range(kv_heads):
        for r in range(rows):
            q = jnp.concatenate([query(m * per + i, r) for i in range(per)], axis=0).astype(BF16)
            s = lax.dot_general(
                q, stored_ref[r, 0, m], (((1,), (1,)), ((), ())), preferred_element_type=F32
            )
            scores_ref[m * group : (m + 1) * group, r, :] = s * scale

    pos = lax.broadcasted_iota(jnp.int32, (rows, span), 1)
    visible = (pos <= limit_ref[...])[None]
    scores = jnp.where(visible, scores_ref[...], -1e30)
    top = jnp.max(scores, axis=-1, keepdims=True)
    weights = jnp.where(visible, jnp.exp(scores - top), 0.0)
    total = jnp.sum(weights, axis=-1, keepdims=True)
    scores_ref[...] = weights

    for m in range(kv_heads):
        for r in range(rows):
            w = scores_ref[m * group : (m + 1) * group, r, :].astype(BF16)
            mixed_ref[m * group : (m + 1) * group, r, :] = jnp.dot(
                w, stored_ref[r, 1, m], preferred_element_type=F32
            )

    n = heads * rows
    for k in range(tp):
        own = slice(k * heads, (k + 1) * heads)
        array, at = place(k, tp)
        outs[array][at] = packed(
            mixed_ref[own].reshape(n, dim),
            to_lanes(top[own].reshape(n, 1)),
            to_lanes(total[own].reshape(n, 1)),
        )


def merge_kernel(after_ref, kept_ref, got_ref, *out_refs):
    del after_ref
    at = 0
    for out_ref in out_refs:
        for i in range(out_ref.shape[0]):
            out_ref[i] = packed(*merged([kept_ref[at], got_ref[at]]))
            at += 1


def requantized(x):
    top = jnp.max(jnp.abs(x), axis=-1, keepdims=True)
    scale = ((top + 1e-06) / 127.0).astype(BF16).astype(F32)
    return jnp.clip(jnp.floor(x / scale + 0.5), -127.0, 127.0) * scale


def project_columns(flat, weight, out_ref, i, start):
    columns = weight.shape[1]
    tile = min(512, columns)
    for c in range(0, columns, tile):
        part = jnp.dot(flat, weight[:, c : c + tile], preferred_element_type=F32)
        for b in range(0, tile, QB):
            at = start + c + b
            block = requantized(part[:, b : b + QB])
            out_ref[i, :, at : at + QB] = block.astype(out_ref.dtype)


def project_units(flat, held, places, out_ref):
    for i, (array, index) in enumerate(places):
        columns = held[array].shape[2]
        project_columns(flat, held[array].at[index], out_ref, i // 2, i % 2 * columns)


def project_away_kernel(rows, heads, places, units, *refs):
    sources, weight_ref, held = refs[:4], refs[4], refs[5:-4]
    flat_ref, out_ref, later_ref, sems = refs[-4:]
    copies = weight_copies(units, weight_ref, later_ref, sems)
    for copy in copies:
        copy.start()
    mixed, _, total = merged([source[0] for source in sources])
    attended = mixed / to_column(total, mixed.shape[0])
    flat = jnp.concatenate(
        [attended[h * rows : (h + 1) * rows] for h in range(heads)], axis=1
    ).astype(BF16)
    flat_ref[...] = flat
    project_units(flat, held, places, out_ref)
    for copy in copies:
        copy.wait()


def project_own_kernel(places, units, flat_ref, weight_ref, *refs):
    held, (out_ref, late_ref, sems) = refs[:-3], refs[-3:]
    copies = weight_copies(units, weight_ref, late_ref, sems)
    for copy in copies:
        copy.start()
    flat = flat_ref[...]
    project_units(flat, held, places, out_ref)
    columns = late_ref.shape[2]
    for i, copy in enumerate(copies, len(places)):
        copy.wait()
        late = late_ref.at[i - len(places)]
        project_columns(flat, late, out_ref, i // 2, i % 2 * columns)


def split_kernel(kept_ref, got_ref, send_ref, keep_ref):
    for i in range(send_ref.shape[0]):
        send_ref[i] = (kept_ref[2 * i + 1] + got_ref[2 * i + 1].astype(F32)).astype(BF16)
        keep_ref[i] = kept_ref[2 * i] + got_ref[2 * i].astype(F32)


def pair_kernel(kept_ref, got_ref, residual_ref, far_ref, even_ref, odd_ref):
    for i in range(4):
        x = kept_ref[i] + got_ref[i].astype(F32)
        if i == 0:
            x = x + residual_ref[0].astype(F32)
        if i & 1:
            odd_ref[i >> 1] = x.astype(BF16)
            far_ref[i >> 1] = x.astype(BF16)
        else:
            even_ref[i >> 1] = x.astype(BF16)


def owner_kernel(three_ref, two_ref, one_ref, near_ref, out_ref):
    for i in range(2):
        for b in range(0, out_ref.shape[2], QB):
            at = slice(b, b + QB)
            x = near_ref[i, :, at].astype(F32) + one_ref[i, :, at].astype(F32)
            y = two_ref[1 - i, :, at].astype(F32) + three_ref[1 - i, :, at].astype(F32)
            out_ref[i, :, at] = requantized(x + y).astype(BF16)


def place_kernel(offsets, high, *refs):
    blocks, out_ref = refs[:-1], refs[-1]
    width = blocks[0].shape[2]
    rank = lax.axis_index("tp")
    for offset, block in zip(offsets, blocks):
        for i in range(2):
            start = pl.multiple_of((rank ^ offset ^ (i * high)) * width, width)
            out_ref[0, :, pl.ds(start, width)] = block[i]


def call(kernel, name, outs, args, in_specs=None, scratch=(), mib=4, cost=MIB):
    return pl.pallas_call(
        kernel,
        out_shape=outs,
        in_specs=in_specs or [VMEM_SPEC] * len(args),
        out_specs=jax.tree.map(lambda _: VMEM_SPEC, outs),
        scratch_shapes=scratch,
        compiler_params=pltpu.CompilerParams(vmem_limit_bytes=mib * MIB),
        cost_estimate=pl.CostEstimate(flops=cost, bytes_accessed=cost, transcendentals=0),
        name=name,
    )(*args)


def in_hbm(array):
    return pltpu.with_memory_space_constraint(array, pltpu.HBM)


def local(tp, sections, queries, new_kv, kv_cache, lengths, residual, out_weight):
    rows, heads, dim = queries.shape[1:]
    kv_heads, span = kv_cache.shape[3:5]
    depth, full = out_weight.shape[1:]
    width = full // tp
    half = tp // 2
    bits = tp.bit_length() - 1
    struct = jax.ShapeDtypeStruct

    def exchanged(array, k, shift=0):
        pairs = [
            (s * tp + t, ((s + shift) % sections) * tp + (t ^ k))
            for s in range(sections)
            for t in range(tp)
        ]
        return lax.ppermute(array, ("section", "tp"), pairs)

    weight = in_hbm(out_weight)
    quarter = tp // 4
    groups = [g * quarter for g in range(1, 4)]
    order = [(slot, h) for slot in (*range(1, tp, 2), *range(0, tp, 2)) for h in range(2)]
    each = tp // 8
    staged = []

    def next_units(count):
        used = sum(len(units) for units, _ in staged)
        return order[used : used + count * each]

    def held_shape(units):
        return pltpu.VMEM((len(units), depth, width // 2), BF16)

    def stage(after, count):
        units = next_units(count)
        held = call(
            functools.partial(stage_kernel, units),
            "stage",
            held_shape(units),
            (weight, after),
            in_specs=[ANY_SPEC, VMEM_SPEC],
            scratch=[pltpu.SemaphoreType.DMA((len(units),))],
            cost=2 * MIB * count,
        )
        staged.append((units, held))
        return held

    got = exchanged(queries, 1)
    units = next_units(2)
    stored, limit, have, held = call(
        functools.partial(stage_cache_kernel, tp // kv_heads, units),
        "stage_cache",
        [
            pltpu.VMEM(kv_cache.shape[1:], BF16),
            pltpu.VMEM((rows, span), jnp.int32),
            pltpu.VMEM(queries.shape, BF16),
            held_shape(units),
        ],
        (in_hbm(lengths), in_hbm(new_kv), in_hbm(kv_cache), in_hbm(queries), weight),
        in_specs=[ANY_SPEC] * 5,
        scratch=[
            pltpu.SMEM(lengths.shape, jnp.int32),
            pltpu.VMEM(new_kv.shape[1:], BF16),
            pltpu.VMEM(kv_cache.shape[1:], BF16),
            pltpu.SemaphoreType.DMA((4,)),
            pltpu.SemaphoreType.DMA((len(units),)),
        ],
        cost=8 * MIB,
    )
    staged.append((units, held))
    after = limit
    for b in range(bits - 2):
        count = 2 << b
        have = call(
            append_kernel, "append", struct((count, rows, heads, dim), BF16), (after, have, got)
        )
        after = have
        if b < bits - 3:
            got = exchanged(have, 2 << b)
    all_queries = [have, *(exchanged(have, k) for k in reversed(groups))]
    all_queries[1:] = all_queries[:0:-1]
    after = stage(have, 2)
    packed_block = (heads * rows + STAT_ROWS, dim)
    kept, send = call(
        attention_kernel,
        "attention",
        [struct((half, *packed_block), BF16)] * 2,
        (stored, limit, after, *all_queries),
        scratch=[pltpu.VMEM((heads * tp, rows, span), F32)] * 2,
        cost=8 * MIB,
    )
    got = exchanged(send, quarter // 2)
    after = stage(send, 4)
    for b in reversed(range(bits - 3)):
        kept, send = call(
            merge_kernel, "merge", [struct((4 << b, *packed_block), BF16)] * 2, (after, kept, got)
        )
        got = exchanged(send, 1 << b)
        after = send
    pending = call(
        merge_kernel, "merge", [struct((1, *packed_block), BF16)] * 4, (after, kept, got)
    )
    last = pending[3]
    pending = [pending[0], *(exchanged(block, k) for block, k in zip(pending[1:], groups[::-1]))]
    stage(last, 4)

    held = [array for _, array in staged]
    places = [(a, i) for a, (units, _) in enumerate(staged) for i in range(len(units))]
    units = next_units(2)
    flat, away, later = call(
        functools.partial(project_away_kernel, rows, heads, places[:tp], units),
        "project_away",
        [struct((rows, depth), BF16), struct((half, rows, width), BF16), held_shape(units)],
        (*pending, weight, *held),
        in_specs=[VMEM_SPEC] * 4 + [ANY_SPEC] + [VMEM_SPEC] * len(held),
        scratch=[pltpu.SemaphoreType.DMA((len(units),))],
        cost=16 * MIB,
    )
    got = exchanged(away, 1)
    places += [(len(held), i) for i in range(len(units))]
    held.append(later)
    late = order[len(places) :]
    kept = call(
        functools.partial(project_own_kernel, places[tp:], late),
        "project_own",
        struct((half, rows, width), F32),
        (flat, weight, *held),
        in_specs=[VMEM_SPEC, ANY_SPEC] + [VMEM_SPEC] * len(held),
        scratch=[
            pltpu.VMEM((len(late), depth, width // 2), BF16),
            pltpu.SemaphoreType.DMA((len(late),)),
        ],
        mib=14,
        cost=16 * MIB,
    )
    for b in range(1, bits - 2):
        slots = kept.shape[0] // 2
        send, kept = call(
            split_kernel,
            "split_sum",
            [struct((slots, rows, width), BF16), struct((slots, rows, width), F32)],
            (kept, got),
        )
        got = exchanged(send, 1 << b)
    far, even, odd = call(
        pair_kernel, "pair_sum", [struct((2, rows, width), BF16)] * 3, (kept, got, residual)
    )
    three = exchanged(far, groups[2])
    two = exchanged(even, groups[1])
    one = exchanged(odd, groups[0])
    own = call(
        owner_kernel, "owner", struct((2, rows, width), BF16), (three, two, one, even)
    )
    high = 1 << (bits - 1)
    parts = [(k, exchanged(own, k, 1)) for k in range(high)]
    return call(
        functools.partial(place_kernel, [offset for offset, _ in parts], high),
        "placed",
        struct((1, rows, full), BF16),
        [part for _, part in parts],
    )


def solution(mesh):
    return jax.shard_map(
        functools.partial(local, mesh.shape["tp"], mesh.shape["section"]),
        mesh=mesh,
        in_specs=(
            P("section", "rep", "tp", None),
            P("section", "rep", None, None, None),
            P("section", "rep", None, None, "tp", None),
            P("section", "rep"),
            P("section", "rep", "tp"),
            P("section", "tp", None),
        ),
        out_specs=P("section", "rep", None),
        check_vma=False,
    )
```

```python
import functools
import math

import jax
import jax.numpy as jnp
from jax import lax
from jax.experimental import pallas as pl
from jax.experimental.pallas import tpu as pltpu
from jax.sharding import PartitionSpec as P

QB = 128
LANES = 128
STAT_ROWS = 16
MIB = 1 << 20
F32 = jnp.float32
BF16 = jnp.bfloat16
VMEM_SPEC = pl.BlockSpec(memory_space=pltpu.VMEM)
ANY_SPEC = pl.BlockSpec(memory_space=pl.ANY)


def pieces(x):
    high = x.astype(BF16).astype(F32)
    rest = x - high
    middle = rest.astype(BF16).astype(F32)
    return high, middle, rest - middle


def weight_copies(units, weight_ref, held_ref, sems):
    rank = lax.axis_index("tp")
    columns = held_ref.shape[2]
    copies = []
    for i, (slot, half) in enumerate(units):
        start = pl.multiple_of(((rank ^ slot) * 2 + half) * columns, columns)
        copies.append(
            pltpu.make_async_copy(
                weight_ref.at[0, :, pl.ds(start, columns)], held_ref.at[i], sems.at[i]
            )
        )
    return copies


def stage_cache_kernel(
    per, units, lengths_ref, new_ref, kv_ref, queries_ref, weight_ref,
    stored_ref, limit_ref, near_ref, held_ref, lengths, new, kv, sems, held_sems,
):
    rank = lax.axis_index("tp")
    rows, _, kv_heads, span, dim = kv.shape
    copies = [
        pltpu.make_async_copy(lengths_ref, lengths, sems.at[0]),
        pltpu.make_async_copy(new_ref.at[0], new, sems.at[1]),
        pltpu.make_async_copy(kv_ref.at[0], kv, sems.at[2]),
        pltpu.make_async_copy(queries_ref, near_ref, sems.at[3]),
    ]
    held = weight_copies(units, weight_ref, held_ref, held_sems)
    for copy in copies + held:
        copy.start()
    for copy in copies:
        copy.wait()
    first = rank * span
    sub = lax.broadcasted_iota(jnp.int32, (span, dim), 0)
    kv_sub = lax.broadcasted_iota(jnp.int32, (kv_heads, dim), 0)
    row_of = lax.broadcasted_iota(jnp.int32, (rows, span), 0)
    limit = jnp.zeros((rows, span), jnp.int32)
    for r in range(rows):
        limit = jnp.where(row_of == r, lengths[0, r] - first, limit)
        written = sub == lengths[0, r] - first
        for which in range(2):
            new_heads = new[r, which].astype(F32)
            for m in range(kv_heads):
                head = (rank // per) ^ m
                fresh = jnp.sum(
                    jnp.where(kv_sub == head, new_heads, 0.0), axis=0, keepdims=True
                )
                block = kv[r, which, head].astype(F32)
                stored_ref[r, which, m] = jnp.where(written, fresh, block).astype(BF16)
    limit_ref[...] = limit
    for copy in held:
        copy.wait()


def stage_kernel(units, weight_ref, after_ref, held_ref, sems):
    del after_ref
    copies = weight_copies(units, weight_ref, held_ref, sems)
    for copy in copies:
        copy.start()
    for copy in copies:
        copy.wait()


def append_kernel(after_ref, *refs):
    del after_ref
    parts, out_ref = refs[:-1], refs[-1]
    at = 0
    for part in parts:
        out_ref[at : at + part.shape[0]] = part[...]
        at += part.shape[0]


def packed(mixed, top, total):
    stat_sub = lax.broadcasted_iota(jnp.int32, (STAT_ROWS, LANES), 0)
    tile = jnp.zeros((STAT_ROWS, LANES), F32)
    for i, piece in enumerate(pieces(top) + pieces(total)):
        tile = jnp.where(stat_sub == i, piece, tile)
    return jnp.concatenate([mixed, tile], axis=0).astype(BF16)


def to_lanes(column):
    n = column.shape[0]
    sub = lax.broadcasted_iota(jnp.int32, (n, LANES), 0)
    lane = lax.broadcasted_iota(jnp.int32, (n, LANES), 1)
    return jnp.sum(jnp.where(lane == sub, column, 0.0), axis=0, keepdims=True)


def to_column(row, n):
    sub = lax.broadcasted_iota(jnp.int32, (n, LANES), 0)
    lane = lax.broadcasted_iota(jnp.int32, (n, LANES), 1)
    return jnp.sum(jnp.where(lane == sub, row, 0.0), axis=1, keepdims=True)


def merged(blocks):
    n = blocks[0].shape[0] - STAT_ROWS
    tops, sums = [], []
    for block in blocks:
        tile = block[n:].astype(F32)
        tops.append(tile[0:1] + tile[1:2] + tile[2:3])
        sums.append(tile[3:4] + tile[4:5] + tile[5:6])
    top = functools.reduce(jnp.maximum, tops)
    mixed, total = 0.0, 0.0
    for block, own_top, own_sum in zip(blocks, tops, sums):
        factor = jnp.exp(own_top - top)
        total = total + own_sum * factor
        mixed = mixed + block[:n].astype(F32) * to_column(factor, n)
    return mixed, top, total


def place(k, tp):
    quarter = tp // 4
    at = k % quarter * 4 + (4 - k // quarter) % 4
    return at // (tp // 2), at % (tp // 2)


def attention_kernel(stored_ref, limit_ref, after_ref, *refs):
    del after_ref
    sources, outs, (scores_ref, mixed_ref) = refs[:2], refs[2:4], refs[4:]
    half, rows, heads, dim = sources[0].shape
    tp = 2 * half
    kv_heads, span = stored_ref.shape[2:4]
    group = heads * tp // kv_heads
    per = group // heads
    scale = 1.0 / math.sqrt(dim)

    def query(k, r):
        array, at = place(k, tp)
        return sources[array][at, r].astype(F32)

    for m in range(kv_heads):
        for r in range(rows):
            q = jnp.concatenate([query(m * per + i, r) for i in range(per)], axis=0).astype(BF16)
            s = lax.dot_general(
                q, stored_ref[r, 0, m], (((1,), (1,)), ((), ())), preferred_element_type=F32
            )
            scores_ref[m * group : (m + 1) * group, r, :] = s * scale

    pos = lax.broadcasted_iota(jnp.int32, (rows, span), 1)
    visible = (pos <= limit_ref[...])[None]
    scores = jnp.where(visible, scores_ref[...], -1e30)
    top = jnp.max(scores, axis=-1, keepdims=True)
    weights = jnp.where(visible, jnp.exp(scores - top), 0.0)
    total = jnp.sum(weights, axis=-1, keepdims=True)
    scores_ref[...] = weights

    for m in range(kv_heads):
        for r in range(rows):
            w = scores_ref[m * group : (m + 1) * group, r, :].astype(BF16)
            mixed_ref[m * group : (m + 1) * group, r, :] = jnp.dot(
                w, stored_ref[r, 1, m], preferred_element_type=F32
            )

    n = heads * rows
    for k in range(tp):
        own = slice(k * heads, (k + 1) * heads)
        array, at = place(k, tp)
        outs[array][at] = packed(
            mixed_ref[own].reshape(n, dim),
            to_lanes(top[own].reshape(n, 1)),
            to_lanes(total[own].reshape(n, 1)),
        )


def merge_kernel(after_ref, kept_ref, got_ref, *out_refs):
    del after_ref
    at = 0
    for out_ref in out_refs:
        for i in range(out_ref.shape[0]):
            out_ref[i] = packed(*merged([kept_ref[at], got_ref[at]]))
            at += 1


def requantized(x):
    top = jnp.max(jnp.abs(x), axis=-1, keepdims=True)
    scale = ((top + 1e-06) / 127.0).astype(BF16).astype(F32)
    return jnp.clip(jnp.floor(x / scale + 0.5), -127.0, 127.0) * scale


def project_columns(flat, weight, out_ref, i, start):
    columns = weight.shape[1]
    tile = min(512, columns)
    for c in range(0, columns, tile):
        part = jnp.dot(flat, weight[:, c : c + tile], preferred_element_type=F32)
        for b in range(0, tile, QB):
            at = start + c + b
            block = requantized(part[:, b : b + QB])
            out_ref[i, :, at : at + QB] = block.astype(out_ref.dtype)


def project_units(flat, held, places, out_ref):
    for i, (array, index) in enumerate(places):
        columns = held[array].shape[2]
        project_columns(flat, held[array].at[index], out_ref, i // 2, i % 2 * columns)


def project_away_kernel(rows, heads, places, units, *refs):
    sources, weight_ref, held = refs[:4], refs[4], refs[5:-4]
    flat_ref, out_ref, later_ref, sems = refs[-4:]
    copies = weight_copies(units, weight_ref, later_ref, sems)
    for copy in copies:
        copy.start()
    mixed, _, total = merged([source[0] for source in sources])
    attended = mixed / to_column(total, mixed.shape[0])
    flat = jnp.concatenate(
        [attended[h * rows : (h + 1) * rows] for h in range(heads)], axis=1
    ).astype(BF16)
    flat_ref[...] = flat
    project_units(flat, held, places, out_ref)
    for copy in copies:
        copy.wait()


def project_own_kernel(places, units, flat_ref, weight_ref, *refs):
    held, (out_ref, late_ref, sems) = refs[:-3], refs[-3:]
    copies = weight_copies(units, weight_ref, late_ref, sems)
    for copy in copies:
        copy.start()
    flat = flat_ref[...]
    project_units(flat, held, places, out_ref)
    columns = late_ref.shape[2]
    for i, copy in enumerate(copies, len(places)):
        copy.wait()
        late = late_ref.at[i - len(places)]
        project_columns(flat, late, out_ref, i // 2, i % 2 * columns)


def split_kernel(kept_ref, got_ref, send_ref, keep_ref):
    for i in range(send_ref.shape[0]):
        send_ref[i] = (kept_ref[2 * i + 1] + got_ref[2 * i + 1].astype(F32)).astype(BF16)
        keep_ref[i] = kept_ref[2 * i] + got_ref[2 * i].astype(F32)


def pair_kernel(kept_ref, got_ref, residual_ref, far_ref, even_ref, odd_ref):
    for i in range(4):
        x = kept_ref[i] + got_ref[i].astype(F32)
        if i == 0:
            x = x + residual_ref[0].astype(F32)
        if i & 1:
            odd_ref[i >> 1] = x.astype(BF16)
            far_ref[i >> 1] = x.astype(BF16)
        else:
            even_ref[i >> 1] = x.astype(BF16)


def owner_kernel(three_ref, two_ref, one_ref, near_ref, out_ref):
    for i in range(2):
        for b in range(0, out_ref.shape[2], QB):
            at = slice(b, b + QB)
            x = near_ref[i, :, at].astype(F32) + one_ref[i, :, at].astype(F32)
            y = two_ref[1 - i, :, at].astype(F32) + three_ref[1 - i, :, at].astype(F32)
            out_ref[i, :, at] = requantized(x + y).astype(BF16)


def place_kernel(offsets, high, *refs):
    blocks, out_ref = refs[:-1], refs[-1]
    width = blocks[0].shape[2]
    rank = lax.axis_index("tp")
    for offset, block in zip(offsets, blocks):
        for i in range(2):
            start = pl.multiple_of((rank ^ offset ^ (i * high)) * width, width)
            out_ref[0, :, pl.ds(start, width)] = block[i]


def call(kernel, name, outs, args, in_specs=None, scratch=(), mib=4, cost=MIB):
    return pl.pallas_call(
        kernel,
        out_shape=outs,
        in_specs=in_specs or [VMEM_SPEC] * len(args),
        out_specs=jax.tree.map(lambda _: VMEM_SPEC, outs),
        scratch_shapes=scratch,
        compiler_params=pltpu.CompilerParams(vmem_limit_bytes=mib * MIB),
        cost_estimate=pl.CostEstimate(flops=cost, bytes_accessed=cost, transcendentals=0),
        name=name,
    )(*args)


def in_hbm(array):
    return pltpu.with_memory_space_constraint(array, pltpu.HBM)


def local(tp, sections, queries, new_kv, kv_cache, lengths, residual, out_weight):
    rows, heads, dim = queries.shape[1:]
    kv_heads, span = kv_cache.shape[3:5]
    depth, full = out_weight.shape[1:]
    width = full // tp
    half = tp // 2
    bits = tp.bit_length() - 1
    struct = jax.ShapeDtypeStruct

    def exchanged(array, k, shift=0):
        pairs = [
            (s * tp + t, ((s + shift) % sections) * tp + (t ^ k))
            for s in range(sections)
            for t in range(tp)
        ]
        return lax.ppermute(array, ("section", "tp"), pairs)

    weight = in_hbm(out_weight)
    quarter = tp // 4
    groups = [g * quarter for g in range(1, 4)]
    order = [(slot, h) for slot in (*range(1, tp, 2), *range(0, tp, 2)) for h in range(2)]
    each = tp // 8
    staged = []

    def next_units(count):
        used = sum(len(units) for units, _ in staged)
        return order[used : used + count * each]

    def held_shape(units):
        return pltpu.VMEM((len(units), depth, width // 2), BF16)

    def stage(after, count):
        units = next_units(count)
        held = call(
            functools.partial(stage_kernel, units),
            "stage",
            held_shape(units),
            (weight, after),
            in_specs=[ANY_SPEC, VMEM_SPEC],
            scratch=[pltpu.SemaphoreType.DMA((len(units),))],
            cost=2 * MIB * count,
        )
        staged.append((units, held))
        return held

    got = [exchanged(queries, k) for k in groups[::-1]]
    units = next_units(2)
    stored, limit, have, held = call(
        functools.partial(stage_cache_kernel, tp // kv_heads, units),
        "stage_cache",
        [
            pltpu.VMEM(kv_cache.shape[1:], BF16),
            pltpu.VMEM((rows, span), jnp.int32),
            pltpu.VMEM(queries.shape, BF16),
            held_shape(units),
        ],
        (in_hbm(lengths), in_hbm(new_kv), in_hbm(kv_cache), in_hbm(queries), weight),
        in_specs=[ANY_SPEC] * 5,
        scratch=[
            pltpu.SMEM(lengths.shape, jnp.int32),
            pltpu.VMEM(new_kv.shape[1:], BF16),
            pltpu.VMEM(kv_cache.shape[1:], BF16),
            pltpu.SemaphoreType.DMA((4,)),
            pltpu.SemaphoreType.DMA((len(units),)),
        ],
        cost=8 * MIB,
    )
    staged.append((units, held))
    have, after = [have, *got], limit
    for b in range(bits - 2):
        after = call(
            append_kernel, "append", struct((4 << b, rows, heads, dim), BF16), (after, *have)
        )
        have = [after, exchanged(after, 1 << b)]
    after = stage(after, 3)
    packed_block = (heads * rows + STAT_ROWS, dim)
    kept, send = call(
        attention_kernel,
        "attention",
        [struct((half, *packed_block), BF16)] * 2,
        (stored, limit, after, *have),
        scratch=[pltpu.VMEM((heads * tp, rows, span), F32)] * 2,
        cost=8 * MIB,
    )
    got = exchanged(send, quarter // 2)
    after = stage(send, 4)
    for b in reversed(range(bits - 3)):
        kept, send = call(
            merge_kernel, "merge", [struct((4 << b, *packed_block), BF16)] * 2, (after, kept, got)
        )
        got = exchanged(send, 1 << b)
        after = send
    pending = call(
        merge_kernel, "merge", [struct((1, *packed_block), BF16)] * 4, (after, kept, got)
    )
    last = pending[3]
    pending = [pending[0], *(exchanged(block, k) for block, k in zip(pending[1:], groups[::-1]))]
    stage(last, 3)

    held = [array for _, array in staged]
    places = [(a, i) for a, (units, _) in enumerate(staged) for i in range(len(units))]
    units = next_units(2)
    flat, away, later = call(
        functools.partial(project_away_kernel, rows, heads, places[:tp], units),
        "project_away",
        [struct((rows, depth), BF16), struct((half, rows, width), BF16), held_shape(units)],
        (*pending, weight, *held),
        in_specs=[VMEM_SPEC] * 4 + [ANY_SPEC] + [VMEM_SPEC] * len(held),
        scratch=[pltpu.SemaphoreType.DMA((len(units),))],
        cost=16 * MIB,
    )
    got = exchanged(away, 1)
    places += [(len(held), i) for i in range(len(units))]
    held.append(later)
    late = order[len(places) :]
    kept = call(
        functools.partial(project_own_kernel, places[tp:], late),
        "project_own",
        struct((half, rows, width), F32),
        (flat, weight, *held),
        in_specs=[VMEM_SPEC, ANY_SPEC] + [VMEM_SPEC] * len(held),
        scratch=[
            pltpu.VMEM((len(late), depth, width // 2), BF16),
            pltpu.SemaphoreType.DMA((len(late),)),
        ],
        mib=14,
        cost=16 * MIB,
    )
    for b in range(1, bits - 2):
        slots = kept.shape[0] // 2
        send, kept = call(
            split_kernel,
            "split_sum",
            [struct((slots, rows, width), BF16), struct((slots, rows, width), F32)],
            (kept, got),
        )
        got = exchanged(send, 1 << b)
    far, even, odd = call(
        pair_kernel, "pair_sum", [struct((2, rows, width), BF16)] * 3, (kept, got, residual)
    )
    three = exchanged(far, groups[2])
    two = exchanged(even, groups[1])
    one = exchanged(odd, groups[0])
    own = call(
        owner_kernel, "owner", struct((2, rows, width), BF16), (three, two, one, even)
    )
    high = 1 << (bits - 1)
    parts = [(k, exchanged(own, k, 1)) for k in range(high)]
    return call(
        functools.partial(place_kernel, [offset for offset, _ in parts], high),
        "placed",
        struct((1, rows, full), BF16),
        [part for _, part in parts],
    )


def solution(mesh):
    return jax.shard_map(
        functools.partial(local, mesh.shape["tp"], mesh.shape["section"]),
        mesh=mesh,
        in_specs=(
            P("section", "rep", "tp", None),
            P("section", "rep", None, None, None),
            P("section", "rep", None, None, "tp", None),
            P("section", "rep"),
            P("section", "rep", "tp"),
            P("section", "tp", None),
        ),
        out_specs=P("section", "rep", None),
        check_vma=False,
    )
```

```python
import functools
import math

import jax
import jax.numpy as jnp
from jax import lax
from jax.experimental import pallas as pl
from jax.experimental.pallas import tpu as pltpu
from jax.sharding import PartitionSpec as P

QB = 128
LANES = 128
STAT_ROWS = 16
MIB = 1 << 20
F32 = jnp.float32
BF16 = jnp.bfloat16
VMEM_SPEC = pl.BlockSpec(memory_space=pltpu.VMEM)
ANY_SPEC = pl.BlockSpec(memory_space=pl.ANY)


def pieces(x):
    high = x.astype(BF16).astype(F32)
    rest = x - high
    middle = rest.astype(BF16).astype(F32)
    return high, middle, rest - middle


def weight_copies(units, weight_ref, held_ref, sems):
    rank = lax.axis_index("tp")
    columns = held_ref.shape[2]
    copies = []
    for i, (slot, half) in enumerate(units):
        start = pl.multiple_of(((rank ^ slot) * 2 + half) * columns, columns)
        copies.append(
            pltpu.make_async_copy(
                weight_ref.at[0, :, pl.ds(start, columns)], held_ref.at[i], sems.at[i]
            )
        )
    return copies


def stage_cache_kernel(
    per, units, lengths_ref, new_ref, kv_ref, queries_ref, weight_ref,
    stored_ref, limit_ref, near_ref, held_ref, lengths, new, kv, sems, held_sems,
):
    rank = lax.axis_index("tp")
    rows, _, kv_heads, span, dim = kv.shape
    copies = [
        pltpu.make_async_copy(lengths_ref, lengths, sems.at[0]),
        pltpu.make_async_copy(new_ref.at[0], new, sems.at[1]),
        pltpu.make_async_copy(kv_ref.at[0], kv, sems.at[2]),
        pltpu.make_async_copy(queries_ref, near_ref, sems.at[3]),
    ]
    held = weight_copies(units, weight_ref, held_ref, held_sems)
    for copy in copies + held:
        copy.start()
    for copy in copies:
        copy.wait()
    first = rank * span
    sub = lax.broadcasted_iota(jnp.int32, (span, dim), 0)
    kv_sub = lax.broadcasted_iota(jnp.int32, (kv_heads, dim), 0)
    row_of = lax.broadcasted_iota(jnp.int32, (rows, span), 0)
    limit = jnp.zeros((rows, span), jnp.int32)
    for r in range(rows):
        limit = jnp.where(row_of == r, lengths[0, r] - first, limit)
        written = sub == lengths[0, r] - first
        for which in range(2):
            new_heads = new[r, which].astype(F32)
            for m in range(kv_heads):
                head = (rank // per) ^ m
                fresh = jnp.sum(
                    jnp.where(kv_sub == head, new_heads, 0.0), axis=0, keepdims=True
                )
                block = kv[r, which, head].astype(F32)
                stored_ref[r, which, m] = jnp.where(written, fresh, block).astype(BF16)
    limit_ref[...] = limit
    for copy in held:
        copy.wait()


def stage_kernel(units, weight_ref, after_ref, held_ref, sems):
    del after_ref
    copies = weight_copies(units, weight_ref, held_ref, sems)
    for copy in copies:
        copy.start()
    for copy in copies:
        copy.wait()


def append_kernel(after_ref, *refs):
    del after_ref
    parts, out_ref = refs[:-1], refs[-1]
    at = 0
    for part in parts:
        out_ref[at : at + part.shape[0]] = part[...]
        at += part.shape[0]


def packed(mixed, top, total):
    stat_sub = lax.broadcasted_iota(jnp.int32, (STAT_ROWS, LANES), 0)
    tile = jnp.zeros((STAT_ROWS, LANES), F32)
    for i, piece in enumerate(pieces(top) + pieces(total)):
        tile = jnp.where(stat_sub == i, piece, tile)
    return jnp.concatenate([mixed, tile], axis=0).astype(BF16)


def to_lanes(column):
    n = column.shape[0]
    sub = lax.broadcasted_iota(jnp.int32, (n, LANES), 0)
    lane = lax.broadcasted_iota(jnp.int32, (n, LANES), 1)
    return jnp.sum(jnp.where(lane == sub, column, 0.0), axis=0, keepdims=True)


def to_column(row, n):
    sub = lax.broadcasted_iota(jnp.int32, (n, LANES), 0)
    lane = lax.broadcasted_iota(jnp.int32, (n, LANES), 1)
    return jnp.sum(jnp.where(lane == sub, row, 0.0), axis=1, keepdims=True)


def merged(blocks):
    n = blocks[0].shape[0] - STAT_ROWS
    tops, sums = [], []
    for block in blocks:
        tile = block[n:].astype(F32)
        tops.append(tile[0:1] + tile[1:2] + tile[2:3])
        sums.append(tile[3:4] + tile[4:5] + tile[5:6])
    top = functools.reduce(jnp.maximum, tops)
    mixed, total = 0.0, 0.0
    for block, own_top, own_sum in zip(blocks, tops, sums):
        factor = jnp.exp(own_top - top)
        total = total + own_sum * factor
        mixed = mixed + block[:n].astype(F32) * to_column(factor, n)
    return mixed, top, total


def place(k, tp):
    quarter = tp // 4
    at = k % quarter * 4 + (4 - k // quarter) % 4
    return at // (tp // 2), at % (tp // 2)


def attention_kernel(stored_ref, limit_ref, after_ref, *refs):
    del after_ref
    sources, outs, (scores_ref, mixed_ref) = refs[:4], refs[4:6], refs[6:]
    quarter, rows, heads, dim = sources[0].shape
    tp = 4 * quarter
    kv_heads, span = stored_ref.shape[2:4]
    group = heads * tp // kv_heads
    per = group // heads
    scale = 1.0 / math.sqrt(dim)

    def query(k, r):
        return sources[k // quarter][k % quarter, r].astype(F32)

    for m in range(kv_heads):
        for r in range(rows):
            q = jnp.concatenate([query(m * per + i, r) for i in range(per)], axis=0).astype(BF16)
            s = lax.dot_general(
                q, stored_ref[r, 0, m], (((1,), (1,)), ((), ())), preferred_element_type=F32
            )
            scores_ref[m * group : (m + 1) * group, r, :] = s * scale

    pos = lax.broadcasted_iota(jnp.int32, (rows, span), 1)
    visible = (pos <= limit_ref[...])[None]
    scores = jnp.where(visible, scores_ref[...], -1e30)
    top = jnp.max(scores, axis=-1, keepdims=True)
    weights = jnp.where(visible, jnp.exp(scores - top), 0.0)
    total = jnp.sum(weights, axis=-1, keepdims=True)
    scores_ref[...] = weights

    for m in range(kv_heads):
        for r in range(rows):
            w = scores_ref[m * group : (m + 1) * group, r, :].astype(BF16)
            mixed_ref[m * group : (m + 1) * group, r, :] = jnp.dot(
                w, stored_ref[r, 1, m], preferred_element_type=F32
            )

    n = heads * rows
    for k in range(tp):
        own = slice(k * heads, (k + 1) * heads)
        array, at = place(k, tp)
        outs[array][at] = packed(
            mixed_ref[own].reshape(n, dim),
            to_lanes(top[own].reshape(n, 1)),
            to_lanes(total[own].reshape(n, 1)),
        )


def merge_kernel(after_ref, kept_ref, got_ref, *out_refs):
    del after_ref
    at = 0
    for out_ref in out_refs:
        for i in range(out_ref.shape[0]):
            out_ref[i] = packed(*merged([kept_ref[at], got_ref[at]]))
            at += 1


def requantized(x):
    top = jnp.max(jnp.abs(x), axis=-1, keepdims=True)
    scale = ((top + 1e-06) / 127.0).astype(BF16).astype(F32)
    return jnp.clip(jnp.floor(x / scale + 0.5), -127.0, 127.0) * scale


def project_columns(flat, weight, out_ref, i, start):
    columns = weight.shape[1]
    tile = min(512, columns)
    for c in range(0, columns, tile):
        part = jnp.dot(flat, weight[:, c : c + tile], preferred_element_type=F32)
        for b in range(0, tile, QB):
            at = start + c + b
            block = requantized(part[:, b : b + QB])
            out_ref[i, :, at : at + QB] = block.astype(out_ref.dtype)


def project_units(flat, held, places, out_ref):
    for i, (array, index) in enumerate(places):
        columns = held[array].shape[2]
        project_columns(flat, held[array].at[index], out_ref, i // 2, i % 2 * columns)


def project_away_kernel(rows, heads, places, units, *refs):
    sources, weight_ref, held = refs[:4], refs[4], refs[5:-4]
    flat_ref, out_ref, later_ref, sems = refs[-4:]
    copies = weight_copies(units, weight_ref, later_ref, sems)
    for copy in copies:
        copy.start()
    mixed, _, total = merged([source[0] for source in sources])
    attended = mixed / to_column(total, mixed.shape[0])
    flat = jnp.concatenate(
        [attended[h * rows : (h + 1) * rows] for h in range(heads)], axis=1
    ).astype(BF16)
    flat_ref[...] = flat
    project_units(flat, held, places, out_ref)
    for copy in copies:
        copy.wait()


def project_own_kernel(places, units, flat_ref, weight_ref, *refs):
    held, (out_ref, late_ref, sems) = refs[:-3], refs[-3:]
    copies = weight_copies(units, weight_ref, late_ref, sems)
    for copy in copies:
        copy.start()
    flat = flat_ref[...]
    project_units(flat, held, places, out_ref)
    columns = late_ref.shape[2]
    for i, copy in enumerate(copies, len(places)):
        copy.wait()
        late = late_ref.at[i - len(places)]
        project_columns(flat, late, out_ref, i // 2, i % 2 * columns)


def split_kernel(kept_ref, got_ref, send_ref, keep_ref):
    for i in range(send_ref.shape[0]):
        send_ref[i] = (kept_ref[2 * i + 1] + got_ref[2 * i + 1].astype(F32)).astype(BF16)
        keep_ref[i] = kept_ref[2 * i] + got_ref[2 * i].astype(F32)


def pair_kernel(kept_ref, got_ref, residual_ref, far_ref, even_ref, odd_ref, near_ref):
    for i in range(4):
        x = kept_ref[i] + got_ref[i].astype(F32)
        if i == 0:
            x = x + residual_ref[0].astype(F32)
        if i & 1:
            odd_ref[i >> 1] = x.astype(BF16)
            far_ref[i >> 1] = x.astype(BF16)
        else:
            even_ref[i >> 1] = x.astype(BF16)
            near_ref[i >> 1] = x.astype(BF16)


def owner_kernel(three_ref, two_ref, one_ref, near_ref, out_ref):
    for i in range(2):
        for b in range(0, out_ref.shape[2], QB):
            at = slice(b, b + QB)
            x = near_ref[i, :, at].astype(F32) + one_ref[i, :, at].astype(F32)
            y = two_ref[1 - i, :, at].astype(F32) + three_ref[1 - i, :, at].astype(F32)
            out_ref[i, :, at] = requantized(x + y).astype(BF16)


def place_kernel(offsets, high, *refs):
    blocks, out_ref = refs[:-1], refs[-1]
    width = blocks[0].shape[2]
    rank = lax.axis_index("tp")
    for offset, block in zip(offsets, blocks):
        for i in range(2):
            start = pl.multiple_of((rank ^ offset ^ (i * high)) * width, width)
            out_ref[0, :, pl.ds(start, width)] = block[i]


def call(kernel, name, outs, args, in_specs=None, scratch=(), mib=4, cost=MIB):
    return pl.pallas_call(
        kernel,
        out_shape=outs,
        in_specs=in_specs or [VMEM_SPEC] * len(args),
        out_specs=jax.tree.map(lambda _: VMEM_SPEC, outs),
        scratch_shapes=scratch,
        compiler_params=pltpu.CompilerParams(vmem_limit_bytes=mib * MIB),
        cost_estimate=pl.CostEstimate(flops=cost, bytes_accessed=cost, transcendentals=0),
        name=name,
    )(*args)


def in_hbm(array):
    return pltpu.with_memory_space_constraint(array, pltpu.HBM)


def local(tp, sections, queries, new_kv, kv_cache, lengths, residual, out_weight):
    rows, heads, dim = queries.shape[1:]
    kv_heads, span = kv_cache.shape[3:5]
    depth, full = out_weight.shape[1:]
    width = full // tp
    half = tp // 2
    bits = tp.bit_length() - 1
    struct = jax.ShapeDtypeStruct

    def exchanged(array, k, shift=0):
        pairs = [
            (s * tp + t, ((s + shift) % sections) * tp + (t ^ k))
            for s in range(sections)
            for t in range(tp)
        ]
        return lax.ppermute(array, ("section", "tp"), pairs)

    weight = in_hbm(out_weight)
    quarter = tp // 4
    groups = [g * quarter for g in range(1, 4)]
    order = [(slot, h) for slot in (*range(1, tp, 2), *range(0, tp, 2)) for h in range(2)]
    each = tp // 8
    staged = []

    def next_units(count):
        used = sum(len(units) for units, _ in staged)
        return order[used : used + count * each]

    def held_shape(units):
        return pltpu.VMEM((len(units), depth, width // 2), BF16)

    def stage(after, count):
        units = next_units(count)
        held = call(
            functools.partial(stage_kernel, units),
            "stage",
            held_shape(units),
            (weight, after),
            in_specs=[ANY_SPEC, VMEM_SPEC],
            scratch=[pltpu.SemaphoreType.DMA((len(units),))],
            cost=2 * MIB * count,
        )
        staged.append((units, held))
        return held

    got = exchanged(queries, 1)
    units = next_units(2)
    stored, limit, have, held = call(
        functools.partial(stage_cache_kernel, tp // kv_heads, units),
        "stage_cache",
        [
            pltpu.VMEM(kv_cache.shape[1:], BF16),
            pltpu.VMEM((rows, span), jnp.int32),
            pltpu.VMEM(queries.shape, BF16),
            held_shape(units),
        ],
        (in_hbm(lengths), in_hbm(new_kv), in_hbm(kv_cache), in_hbm(queries), weight),
        in_specs=[ANY_SPEC] * 5,
        scratch=[
            pltpu.SMEM(lengths.shape, jnp.int32),
            pltpu.VMEM(new_kv.shape[1:], BF16),
            pltpu.VMEM(kv_cache.shape[1:], BF16),
            pltpu.SemaphoreType.DMA((4,)),
            pltpu.SemaphoreType.DMA((len(units),)),
        ],
        cost=8 * MIB,
    )
    staged.append((units, held))
    after = limit
    for b in range(bits - 2):
        count = 2 << b
        have = call(
            append_kernel, "append", struct((count, rows, heads, dim), BF16), (after, have, got)
        )
        after = have
        if b < bits - 3:
            got = exchanged(have, 2 << b)
    all_queries = [have, *(exchanged(have, k) for k in reversed(groups))]
    all_queries[1:] = all_queries[:0:-1]
    after = stage(have, 2)
    packed_block = (heads * rows + STAT_ROWS, dim)
    kept, send = call(
        attention_kernel,
        "attention",
        [struct((half, *packed_block), BF16)] * 2,
        (stored, limit, after, *all_queries),
        scratch=[pltpu.VMEM((heads * tp, rows, span), F32)] * 2,
        cost=8 * MIB,
    )
    got = exchanged(send, quarter // 2)
    after = stage(send, 4)
    for b in reversed(range(bits - 3)):
        kept, send = call(
            merge_kernel, "merge", [struct((4 << b, *packed_block), BF16)] * 2, (after, kept, got)
        )
        got = exchanged(send, 1 << b)
        after = send
    pending = call(
        merge_kernel, "merge", [struct((1, *packed_block), BF16)] * 4, (after, kept, got)
    )
    last = pending[3]
    pending = [pending[0], *(exchanged(block, k) for block, k in zip(pending[1:], groups[::-1]))]
    stage(last, 4)

    held = [array for _, array in staged]
    places = [(a, i) for a, (units, _) in enumerate(staged) for i in range(len(units))]
    units = next_units(2)
    flat, away, later = call(
        functools.partial(project_away_kernel, rows, heads, places[:tp], units),
        "project_away",
        [struct((rows, depth), BF16), struct((half, rows, width), BF16), held_shape(units)],
        (*pending, weight, *held),
        in_specs=[VMEM_SPEC] * 4 + [ANY_SPEC] + [VMEM_SPEC] * len(held),
        scratch=[pltpu.SemaphoreType.DMA((len(units),))],
        cost=16 * MIB,
    )
    got = exchanged(away, 1)
    places += [(len(held), i) for i in range(len(units))]
    held.append(later)
    late = order[len(places) :]
    kept = call(
        functools.partial(project_own_kernel, places[tp:], late),
        "project_own",
        struct((half, rows, width), F32),
        (flat, weight, *held),
        in_specs=[VMEM_SPEC, ANY_SPEC] + [VMEM_SPEC] * len(held),
        scratch=[
            pltpu.VMEM((len(late), depth, width // 2), BF16),
            pltpu.SemaphoreType.DMA((len(late),)),
        ],
        mib=14,
        cost=16 * MIB,
    )
    for b in range(1, bits - 2):
        slots = kept.shape[0] // 2
        send, kept = call(
            split_kernel,
            "split_sum",
            [struct((slots, rows, width), BF16), struct((slots, rows, width), F32)],
            (kept, got),
        )
        got = exchanged(send, 1 << b)
    far, even, odd, near = call(
        pair_kernel, "pair_sum", [struct((2, rows, width), BF16)] * 4, (kept, got, residual)
    )
    three = exchanged(far, groups[2])
    two = exchanged(even, groups[1])
    one = exchanged(odd, groups[0])
    own = call(
        owner_kernel, "owner", struct((2, rows, width), BF16), (three, two, one, near)
    )
    high = 1 << (bits - 1)
    parts = [(k, exchanged(own, k, 1)) for k in range(high)]
    return call(
        functools.partial(place_kernel, [offset for offset, _ in parts], high),
        "placed",
        struct((1, rows, full), BF16),
        [part for _, part in parts],
    )


def solution(mesh):
    return jax.shard_map(
        functools.partial(local, mesh.shape["tp"], mesh.shape["section"]),
        mesh=mesh,
        in_specs=(
            P("section", "rep", "tp", None),
            P("section", "rep", None, None, None),
            P("section", "rep", None, None, "tp", None),
            P("section", "rep"),
            P("section", "rep", "tp"),
            P("section", "tp", None),
        ),
        out_specs=P("section", "rep", None),
        check_vma=False,
    )
```
